1024 devices in a mesh: blk: 256 (over z_lo, y, x, core), rep: 4 (over z_hi).
Axes of the slice: x: 8, y: 8, z: 8 (z_hi: 4, z_lo: 2; z = z_hi * 2 + z_lo), core: 2. Of those that a mesh axis runs over, the one named last changes fastest.
Arguments:
- features: bfloat16 [65536, 768], P('blk', 'rep'), may hold values from -6 to 6
- weight: bfloat16 [768, 1024], replicated, may hold values from -0.21875 to 0.21875
- cotangent: bfloat16 [65536, 1024], P('blk', 'rep'), may hold values from -6 to 6
- tile_val: bfloat16 [256, 20, 128, 128], P('blk'), may hold values from -40 to 40
- tile_row: int32 [256, 20], P('blk'), may hold values from 0 to 1
- tile_col: int32 [256, 20], P('blk'), may hold values from 0 to 17
- tile_count: int32 [256], P('blk'), may hold values from 2 to 20, as said below
Outputs:
- hidden: bfloat16 [65536, 1024], P('blk', 'rep')
- weight_grad: float32 [768, 1024], P('rep')
- feature_grad: bfloat16 [65536, 768], P('blk', 'rep')
The draws below stay inside these ranges and needn't reach their ends.
Inputs may be any that keep to these rules, and one draw needn't show every extreme that they name: Slots from tile_count[b] on are ignored; some block fills all 20 slots.
All inputs are finite; a program needn't handle non-finite values.
Results may differ from the reference program's by a relative error of at most 0.015.
Values may be sent and summed in bfloat16 or wider, within the bound.
A program may use at most 32 MiB of HBM per device.

```python
import jax
import jax.numpy as jnp
from jax import lax

F_IN = 768
HID = 1024
TILE = 128
ROWT = 2
REACH = 4
MAXT = 20
BLOCKS = 256
NODES = 65536


def draw_tile_val(key, part):
    key = jax.random.fold_in(key, 4)
    first, second, third = jax.random.split(key, 3)
    shape = (BLOCKS, MAXT, TILE, TILE)
    base = jnp.clip(jax.random.normal(first, shape, jnp.float32), -4.0, 4.0)
    spread = 2.3
    row_scale = jnp.exp(spread * jax.random.uniform(second, (BLOCKS, MAXT, TILE, 1), jnp.float32, -0.5, 0.5))
    col_scale = jnp.exp(spread * jax.random.uniform(third, (BLOCKS, MAXT, 1, TILE), jnp.float32, -0.5, 0.5))
    return (base * row_scale * col_scale).astype(jnp.bfloat16)


def draw_tile_count(key, part):
    key = jax.random.fold_in(key, 7)
    first, second, third = jax.random.split(key, 3)
    light = jax.random.randint(first, (BLOCKS,), ROWT, MAXT // 2 + 1)
    heavy = jax.random.randint(second, (BLOCKS,), 0, 8) == 0
    chosen = jax.random.randint(third, (), 0, BLOCKS)
    counts = jnp.where(heavy, MAXT, light)
    counts = jnp.where(jnp.arange(BLOCKS) == chosen, MAXT, counts)
    return counts.astype(jnp.int32)


def with_ends(values, key, least, largest):
    dims = values.shape
    index_at = [jax.random.randint(jax.random.fold_in(key, axis), (), 0, dims[axis]) for axis in range(len(dims))]
    values = values.at[tuple(index_at)].set(least)
    longest = dims.index(max(dims))
    index_at[longest] = (index_at[longest] + 1) % dims[longest]
    return values.at[tuple(index_at)].set(largest)


def shard_levels(key, dims, cuts, least, high):
    level = 1.0
    for dim, shards_of in cuts:
        heights = jax.random.uniform(jax.random.fold_in(jax.random.fold_in(key, 6), dim), (shards_of,), jnp.float32, least / len(cuts), high / len(cuts))
        level = level * jnp.repeat(jnp.exp(heights), dims[dim] // shards_of).reshape((-1,) + (1,) * (len(dims) - 1 - dim))
    return level


def noise(stream_key, shape, width, limit, cuts=(), dtype=jnp.bfloat16):
    factor_of = shard_levels(stream_key, shape, cuts, -0.22, 0.18) if cuts else 1.0
    result = jax.random.normal(stream_key, shape, jnp.float32) * width * factor_of
    return jnp.minimum(jnp.maximum(result, -limit), limit).astype(dtype)


def setup_inputs(seed: int = 0) -> dict:
    keys = jax.random.split(jax.random.key(seed), 8)
    return {
        "features": noise(keys[0], (NODES, F_IN), 1.0, 6.0, ((0, 256), (1, 4))),
        "weight": noise(keys[1], (F_IN, HID), F_IN ** -0.5, 0.21875),
        "cotangent": noise(keys[2], (NODES, HID), 1.0, 6.0, ((0, 256), (1, 4))),
        "tile_val": draw_tile_val(jax.random.fold_in(keys[7], 71), 0),
        "tile_row": with_ends(jax.random.randint(keys[4], (BLOCKS, MAXT), 0, ROWT), jax.random.fold_in(keys[4], 1), 0, ROWT - 1).astype(jnp.int32),
        "tile_col": with_ends(jax.random.randint(keys[5], (BLOCKS, MAXT), 0, (2 * REACH + 1) * ROWT), jax.random.fold_in(keys[5], 1), 0, ((2 * REACH + 1) * ROWT) - 1).astype(jnp.int32),
        "tile_count": draw_tile_count(jax.random.fold_in(keys[7], 71), 0),
    }


def dsilu(value):
    sig = jax.nn.sigmoid(value)
    return sig * (1.0 + value * (1.0 - sig))

def reference(features, weight, cotangent, tile_val, tile_row, tile_col, tile_count):
    highest = lax.Precision.HIGHEST
    ntile = BLOCKS * ROWT
    row_ids = lax.iota(jnp.int32, ROWT)
    slot_ids = lax.iota(jnp.int32, MAXT)
    xt = features.reshape(ntile, TILE, F_IN)

    def layout(index):
        live = (slot_ids < tile_count[index]).astype(jnp.float32)
        place = (tile_row[index][None, :] == row_ids[:, None]).astype(jnp.float32) * live[None, :]
        gcol = ((index * ROWT + tile_col[index] - REACH * ROWT) % ntile).astype(jnp.int32)
        return (live, place, gcol)

    def forward_block(index):
        live, place, gcol = layout(index)
        vals = tile_val[index].astype(jnp.float32)
        xs = xt[gcol].astype(jnp.float32)
        prod = jnp.einsum('sab,sbf->saf', vals, xs, precision=highest)
        summed = jnp.einsum('rs,saf->raf', place, prod, precision=highest)
        row_sq = jnp.einsum('rs,sa->ra', place, lax.optimization_barrier(jnp.sum(vals * vals, axis=2)), precision=highest)
        return (summed, row_sq)
    summed, row_sq = lax.map(forward_block, lax.iota(jnp.int32, BLOCKS))
    scale = lax.rsqrt(1.0 + row_sq.reshape(NODES, 1))
    agg = (features.astype(jnp.float32) + scale * summed.reshape(NODES, F_IN)).astype(jnp.bfloat16)
    pre = jnp.dot(agg, weight, preferred_element_type=jnp.float32)
    hidden = jax.nn.silu(pre).astype(jnp.bfloat16)
    grad_pre = (cotangent.astype(jnp.float32) * dsilu(pre)).astype(jnp.bfloat16)
    weight_grad = jnp.dot(agg.T, grad_pre, preferred_element_type=jnp.float32) / jnp.sqrt(jnp.float32(NODES))
    back = jnp.dot(grad_pre, weight.T, preferred_element_type=jnp.float32)
    scaled = (scale * back).astype(jnp.bfloat16).reshape(ntile, TILE, F_IN)

    def backward_block(total, index):
        live, place, gcol = layout(index)
        vals = tile_val[index].astype(jnp.float32)
        rows_in = scaled[(index * ROWT + tile_row[index]).astype(jnp.int32)].astype(jnp.float32)
        contrib = jnp.einsum('sab,saf->sbf', vals, rows_in, precision=highest) * live[:, None, None]
        return (total.at[gcol].add(contrib), None)
    start = jnp.zeros((ntile, TILE, F_IN), jnp.float32)
    total, unused = lax.scan(backward_block, start, lax.iota(jnp.int32, BLOCKS))
    feature_grad = (back + total.reshape(NODES, F_IN)).astype(jnp.bfloat16)
    return (hidden, weight_grad, feature_grad)
```

```python
import functools

import jax
import jax.numpy as jnp
from jax import lax
from jax.experimental import pallas as pl
from jax.experimental.pallas import tpu as pltpu
from jax.sharding import PartitionSpec as P

TILE = 128
ROWT = 2
REACH = 4
WIDE = 2 * REACH + 1
ZL, NY, NX, NC = 2, 8, 8, 2
SUB = 16
F32 = jnp.float32
BF16 = jnp.bfloat16


def mm(a, b):
    return jnp.dot(a, b, preferred_element_type=F32)


def mm_nt(a, b):
    return lax.dot_general(a, b, (((1,), (1,)), ((), ())), preferred_element_type=F32)


def remote(src, dst, send, recv, where):
    return pltpu.make_async_remote_copy(
        src_ref=src, dst_ref=dst, send_sem=send, recv_sem=recv,
        device_id=where, device_id_type=pl.DeviceIdType.MESH,
    )


def kernel(
    nodes, slots, reps,
    feat_hbm, weight_hbm, cot_hbm, val_hbm, row_ref, col_ref, count_ref,
    hidden_out, wgrad_out, fgrad_out,
    feat, wx, vals, win, adj, adj_t, scale, acc_lo, acc_e, acc_o,
    aggbuf, agg_t, pre, cotbuf, grad, hidden, back, sl, sh, own_part, parts, backbuf, fgrad,
    core_out, core_in, core_own, y_out, y_in, x_out, x_in, xg, yg,
    local_sem, wx_sem, halo_s, halo_r, cot_s, cot_r, agg_s, agg_r, core_s, core_r,
    y_s, y_r, x_s, x_r, xg_s, xg_r, yg_s, yg_r, cg_s, cg_r, hb_s, hb_r, out_sem,
):
    blk = lax.axis_index("blk")
    rep = lax.axis_index("rep")
    blocks = ZL * NY * NX * NC
    core = blk % NC
    x = (blk // NC) % NX
    y = (blk // (NC * NX)) % NY
    zl = blk // (NC * NX * NY)
    xz = zl * NX + x
    panel = feat.shape[1]
    low = TILE
    pieces, piece_rows, _ = core_out.shape
    x_rows = x_out.shape[1]

    def blk_at(offset):
        return {"blk": (blk + offset + blocks) % blocks}

    def y_at(step):
        return {"blk": ((zl * NY + (y + step) % NY) * NX + x) * NC + core}

    def x_at(step):
        return {"blk": ((zl * NY + y) * NX + (x + step) % NX) * NC + core}

    def xz_at(step):
        g = (xz + step) % (ZL * NX)
        return {"blk": (((g // NX) * NY + y) * NX + g % NX) * NC + core}

    def rep_at(step):
        return {"rep": (rep + step) % reps}

    sibling = {"blk": blk + 1 - 2 * core}
    offsets = [d for d in range(-REACH, REACH + 1) if d != 0]

    barrier = pltpu.get_barrier_semaphore()

    def greet(where):
        pl.semaphore_signal(barrier, inc=1, device_id=where, device_id_type=pl.DeviceIdType.MESH)

    for d in offsets:
        greet(blk_at(d))
    for step in range(1, reps):
        greet(rep_at(step))
    for step in range(1, NY):
        greet(y_at(step))
    for step in range(1, ZL * NX):
        greet(xz_at(step))
    greeted = len(offsets) + reps - 1 + NY - 1 + ZL * NX - 1

    get_feat = pltpu.make_async_copy(feat_hbm, feat, local_sem.at[0])
    get_feat.start()
    get_cot = pltpu.make_async_copy(cot_hbm, cotbuf.at[rep], local_sem.at[1])
    get_cot.start()
    get_vals = pltpu.make_async_copy(val_hbm.at[0], vals, local_sem.at[2])
    get_vals.start()
    get_wx = []
    high = panel - low
    for q in range(reps):
        get_wx.append(
            pltpu.make_async_copy(
                weight_hbm.at[pl.ds(q * panel, panel)], wx.at[q, pl.ds(0, panel)], wx_sem.at[2 * q]
            )
        )
        get_wx.append(
            pltpu.make_async_copy(
                weight_hbm.at[pl.ds(q * panel + low, high)],
                wx.at[q, pl.ds(panel, high)],
                wx_sem.at[2 * q + 1],
            )
        )
    for copy in get_wx:
        copy.start()

    get_feat.wait()
    win[REACH, 0:256, :] = feat[:, 0:low]
    win[REACH, 256:384, 0:high] = feat[0:TILE, low:panel]
    win[REACH, 256:384, high:low] = feat[TILE : 2 * TILE, low:panel]
    get_cot.wait()

    pl.semaphore_wait(barrier, greeted)

    halo = {}
    for d in (4, -4, 3, -3, 2, -2, 1, -1):
        halo[d] = remote(win.at[REACH], win.at[REACH - d], halo_s.at[d + REACH], halo_r.at[REACH - d], blk_at(d))
        halo[d].start()
    rep_steps = [2, 1, 3] if reps == 4 else list(range(1, reps))
    cots = {}
    for step in rep_steps:
        cots[step] = remote(cotbuf.at[rep], cotbuf.at[rep], cot_s.at[step], cot_r.at[step], rep_at(step))
        cots[step].start()

    get_vals.wait()
    count = count_ref[0]
    keys = []
    rows = []
    for s in range(slots):
        alive = s < count
        rows.append(jnp.where(alive, row_ref[0, s], -1))
        keys.append(jnp.where(alive, row_ref[0, s] * (WIDE * ROWT) + col_ref[0, s], -1))

    def one_where(cond):
        return jnp.where(cond, 1.0, 0.0).astype(F32)

    chunk = 32

    @pl.loop(0, TILE // chunk)
    def _(c):
        at = pl.ds(pl.multiple_of(c * chunk, chunk), chunk)
        sums = [jnp.zeros((chunk, TILE), F32) for _ in range(ROWT)]
        for s in range(slots):
            v = vals[s, at, :].astype(F32)
            sq = v * v
            for r in range(ROWT):
                sums[r] = sums[r] + sq * one_where(rows[s] == r)
        for r in range(ROWT):
            row_sq = jnp.sum(sums[r], axis=1, keepdims=True)
            to = pl.ds(pl.multiple_of(r * TILE + c * chunk, chunk), chunk)
            scale[to, :] = jnp.broadcast_to(lax.rsqrt(1.0 + row_sq), (chunk, TILE))

    @pl.loop(0, WIDE)
    def _(j):
        masks = [
            [[one_where(keys[s] == r * (WIDE * ROWT) + j * ROWT + t) for s in range(slots)] for t in range(ROWT)]
            for r in range(ROWT)
        ]

        @pl.loop(0, TILE // chunk)
        def _(c):
            at = pl.ds(pl.multiple_of(c * chunk, chunk), chunk)
            sums = [[jnp.zeros((chunk, TILE), F32) for _ in range(ROWT)] for _ in range(ROWT)]
            for s in range(slots):
                v = vals[s, at, :].astype(F32)
                for r in range(ROWT):
                    for t in range(ROWT):
                        sums[r][t] = sums[r][t] + v * masks[r][t][s]
            for r in range(ROWT):
                to = pl.ds(pl.multiple_of(r * TILE + c * chunk, chunk), chunk)
                for t in range(ROWT):
                    adj[j, to, t * TILE : (t + 1) * TILE] = sums[r][t].astype(BF16)

    for d in (0, 1, -1, 2, -2, 3, -3, 4, -4):
        j = REACH - d
        if d != 0:
            halo[d].wait_recv()
        lo = mm(adj[j], win[j, 0:256, :])
        packed = win[j, 256:384, :]
        even = mm(adj[j, :, 0:TILE], packed)
        odd = mm(adj[j, :, TILE : 2 * TILE], packed)
        if d == 0:
            acc_lo[...] = lo
            acc_e[...] = even
            acc_o[...] = odd
        else:
            acc_lo[...] += lo
            acc_e[...] += even
            acc_o[...] += odd

    left = lax.broadcasted_iota(jnp.int32, (TILE, TILE), 1) < high
    summed_lo = win[REACH, 0:256, :].astype(F32) + scale[...] * acc_lo[...]
    both = scale[...] * (acc_e[...] + pltpu.roll(acc_o[...], high, 1))
    both = jnp.where(left, both[0:TILE], pltpu.roll(both[TILE : 2 * TILE], high, 1))
    summed_hi = win[REACH, 256:384, :].astype(F32) + both
    aggbuf[rep, 0:256, :] = summed_lo.astype(BF16)
    aggbuf[rep, 256:384, :] = summed_hi.astype(BF16)
    aggs = {}
    for step in rep_steps:
        aggs[step] = remote(aggbuf.at[rep], aggbuf.at[rep], agg_s.at[step], agg_r.at[step], rep_at(step))
        aggs[step].start()

    agg_t[0:TILE, :] = summed_lo.T.astype(BF16)
    hi_t = summed_hi.T.astype(BF16)
    agg_t[TILE:panel, 0:TILE] = hi_t[0:high]
    agg_t[TILE:panel, TILE : 2 * TILE] = hi_t[high:low]

    def unpacked(q):
        p = aggbuf[q, 256:384, :].astype(F32)
        hi = jnp.concatenate([jnp.where(left, p, 0.0), jnp.where(left, 0.0, p)], axis=0).astype(BF16)
        return aggbuf[q, 0:256, :], hi

    for copy in get_wx:
        copy.wait()
    groups = pre.shape[0]
    wide = pre.shape[2]

    def add_pre(q, first):
        lo, hi = unpacked(q)
        lhs = jnp.concatenate([lo, hi], axis=1)
        for n in range(groups):
            part = mm(lhs, wx[q, :, n * wide : (n + 1) * wide])
            if first:
                pre[n] = part
            else:
                pre[n] += part

    add_pre(rep, True)

    @pl.loop(0, WIDE)
    def _(j):
        for t in range(ROWT):
            adj_t[j, :, t * 256 : (t + 1) * 256] = adj[j, :, t * TILE : (t + 1) * TILE].astype(F32).T.astype(BF16)

    for step in rep_steps[1:] + rep_steps[:1]:
        aggs[step].wait_recv()
        add_pre((rep + reps - step) % reps, False)
    for step in rep_steps:
        cots[step].wait_recv()

    def grad_at(n):
        v = pre[n]
        sig = jax.nn.sigmoid(v)
        slope = sig * (1.0 + v * (1.0 - sig))
        grad[n] = (cotbuf[n].astype(F32) * slope).astype(BF16)

    def weight_part(n, u, out):
        part = mm(agg_t[...], grad[n]).astype(out.dtype)
        for t in range(wide // TILE):
            for h in range(2):
                out[(u * (wide // TILE) + t) * 2 + h] = part[
                    h * piece_rows : (h + 1) * piece_rows, t * TILE : (t + 1) * TILE
                ]

    half = groups // 2
    for u in range(half):
        n = (1 - core) * half + u
        grad_at(n)
        weight_part(n, u, core_out)
    core_copy = remote(core_out, core_in, core_s.at[0], core_r.at[0], sibling)
    core_copy.start()
    for u in range(half):
        n = core * half + u
        grad_at(n)
        weight_part(n, u, core_own)

    back_sum = mm_nt(grad[0], wx[rep, :, 0:wide])
    for n in range(1, groups):
        back_sum = back_sum + mm_nt(grad[n], wx[rep, :, n * wide : (n + 1) * wide])
    back[...] = back_sum

    core_copy.wait_recv()
    for i in range(pieces):
        total = core_own[i] + core_in[i].astype(F32)
        core_own[i] = total
        y_out[i] = total.astype(BF16)
    ys = []
    for step in (4, 3, 5, 2, 6, 1, 7) if NY == 8 else range(1, NY):
        copy = remote(y_out.at[(y + step) % NY], y_in.at[y], y_s.at[step], y_r.at[step], y_at(step))
        copy.start()
        ys.append(copy)

    back_lo = back[:, 0:TILE]
    back_hi = back[:, TILE : 2 * TILE]
    left2 = lax.broadcasted_iota(jnp.int32, (2 * TILE, TILE), 1) < high
    scaled_hi = scale[...] * back_hi
    sl[...] = (scale[...] * back_lo).astype(BF16)
    sh[0:256, :] = jnp.where(left2, scaled_hi, 0.0).astype(BF16)
    sh[256:512, :] = jnp.where(left2, 0.0, scaled_hi).astype(BF16)

    def parts_of(j):
        at = adj_t[j]
        return mm(at[:, 0:256], sl[...]), mm(at[:, 256:512], sl[...]), mm(at, sh[...])

    hbs = []
    for d in (4, -4, 3, -3, 2, -2, 1, -1):
        j = REACH + d
        for i, part in enumerate(parts_of(j)):
            parts[j, i * TILE : (i + 1) * TILE, :] = part.astype(BF16)
        copy = remote(parts.at[j], backbuf.at[REACH - d], hb_s.at[d + REACH], hb_r.at[REACH - d], blk_at(d))
        copy.start()
        hbs.append(copy)
    a, b, c = parts_of(REACH)
    own_part[0:TILE, :] = a + back_lo[0:TILE]
    own_part[TILE : 2 * TILE, :] = b + back_lo[TILE : 2 * TILE]
    own_part[2 * TILE : 3 * TILE, :] = c + jnp.where(left, back_hi[0:TILE], back_hi[TILE : 2 * TILE])

    v = pre[rep]
    hidden[...] = (v * jax.nn.sigmoid(v)).astype(BF16)
    put_hidden = pltpu.make_async_copy(hidden, hidden_out, out_sem.at[0])
    put_hidden.start()

    for copy in ys:
        copy.wait_recv()
    total = core_own[y]
    for step in range(1, NY):
        total = total + y_in[(y + step) % NY].astype(F32)
    filled = piece_rows // x_rows
    x_out[0:filled] = total.astype(BF16).reshape(filled, x_rows, TILE)
    if filled < NX:
        x_out[filled:NX] = jnp.zeros((NX - filled, x_rows, TILE), BF16)
    xs = []
    for step in range(1, ZL * NX):
        to = ((xz + step) % (ZL * NX)) % NX
        copy = remote(x_out.at[to], x_in.at[xz], x_s.at[step], x_r.at[step], xz_at(step))
        copy.start()
        xs.append(copy)
    x_in[xz] = x_out[x]
    for copy in xs:
        copy.wait_recv()
    total = x_in[0].astype(F32)
    for g in range(1, ZL * NX):
        total = total + x_in[g].astype(F32)
    xg[x] = (total * nodes ** -0.5).astype(BF16)
    xgs = []
    for step in range(1, NX):
        copy = remote(xg.at[x], xg.at[x], xg_s.at[step], xg_r.at[step], x_at(step))
        copy.start()
        xgs.append(copy)
    for copy in xgs:
        copy.wait_recv()
    yg[y] = xg[0:filled].reshape(piece_rows, TILE)
    ygs = []
    for step in (4, 3, 5, 2, 6, 1, 7) if NY == 8 else range(1, NY):
        copy = remote(yg.at[y], yg.at[y], yg_s.at[step], yg_r.at[step], y_at(step))
        copy.start()
        ygs.append((step, copy))
    cgs = []

    def pass_on(at, step):
        copy = remote(yg.at[at], wgrad_out.at[core, at], cg_s.at[step], cg_r.at[step], sibling)
        copy.start()
        cgs.append(copy)

    pass_on(y, 0)

    for copy in hbs:
        copy.wait_recv()
    total = own_part[...]
    for d in offsets:
        total = total + backbuf[REACH + d].astype(F32)
    fgrad[...] = total.astype(BF16)
    put_fgrad = pltpu.make_async_copy(fgrad, fgrad_out, out_sem.at[1])
    put_fgrad.start()

    for step, copy in sorted(ygs, key=lambda pair: min(pair[0], NY - pair[0])):
        copy.wait_recv()
        pass_on((y + NY - step) % NY, step)
    put_wgrad = pltpu.make_async_copy(yg, wgrad_out.at[core], out_sem.at[2])
    put_wgrad.start()
    for copy in cgs:
        copy.wait()
    put_hidden.wait()
    put_fgrad.wait()
    put_wgrad.wait()
    for copy in list(halo.values()) + list(cots.values()) + list(aggs.values()) + [core_copy] + ys + hbs + xs + xgs:
        copy.wait_send()
    for _, copy in ygs:
        copy.wait_send()


def body(features, weight, cotangent, tile_val, tile_row, tile_col, tile_count):
    rows, panel = features.shape
    slots = tile_val.shape[1]
    reps = lax.axis_size("rep")
    nodes = rows * lax.axis_size("blk")
    f_in, hid = weight.shape
    wide = cotangent.shape[1]
    pieces = hid // TILE
    piece_rows = panel // 2
    x_rows = SUB * (-(-piece_rows // (SUB * NX)))
    group = ZL * NX
    vmem = pltpu.VMEM
    dma = pltpu.SemaphoreType.DMA
    scratch = [
        vmem((rows, panel), BF16),
        vmem((reps, 2 * TILE, hid), BF16),
        vmem((slots, TILE, TILE), BF16),
        vmem((WIDE, 3 * TILE, TILE), BF16),
        vmem((WIDE, rows, 2 * TILE), BF16),
        vmem((WIDE, TILE, 2 * rows), BF16),
        vmem((rows, TILE), F32),
        vmem((rows, TILE), F32),
        vmem((rows, TILE), F32),
        vmem((rows, TILE), F32),
        vmem((reps, 3 * TILE, TILE), BF16),
        vmem((panel, rows), BF16),
        vmem((reps, rows, wide), F32),
        vmem((reps, rows, wide), BF16),
        vmem((reps, rows, wide), BF16),
        vmem((rows, wide), BF16),
        vmem((rows, 2 * TILE), F32),
        vmem((rows, TILE), BF16),
        vmem((2 * rows, TILE), BF16),
        vmem((3 * TILE, TILE), F32),
        vmem((WIDE, 3 * TILE, TILE), BF16),
        vmem((WIDE, 3 * TILE, TILE), BF16),
        vmem((3 * TILE, TILE), BF16),
        vmem((pieces, piece_rows, TILE), BF16),
        vmem((pieces, piece_rows, TILE), BF16),
        vmem((pieces, piece_rows, TILE), F32),
        vmem((pieces, piece_rows, TILE), BF16),
        vmem((pieces, piece_rows, TILE), BF16),
        vmem((NX, x_rows, TILE), BF16),
        vmem((group, x_rows, TILE), BF16),
        vmem((NX, x_rows, TILE), BF16),
        vmem((pieces, piece_rows, TILE), BF16),
    ] + [
        dma((n,))
        for n in (
            3, 2 * reps, WIDE, WIDE, reps, reps, reps, reps, 1, 1,
            NY, NY, group, group, NX, NX, NY, NY, NY, NY, WIDE, WIDE, 3,
        )
    ]
    anywhere = pl.BlockSpec(memory_space=pl.ANY)
    scalar = pl.BlockSpec(memory_space=pltpu.SMEM)
    hidden, wgrad, fgrad = pl.pallas_call(
        functools.partial(kernel, nodes, slots, reps),
        out_shape=(
            jax.ShapeDtypeStruct((rows, wide), BF16),
            jax.ShapeDtypeStruct((2, pieces, piece_rows, TILE), BF16),
            jax.ShapeDtypeStruct((3 * TILE, TILE), BF16),
        ),
        in_specs=[anywhere] * 4 + [scalar] * 3,
        out_specs=(anywhere,) * 3,
        scratch_shapes=scratch,
        compiler_params=pltpu.CompilerParams(
            collective_id=0, has_side_effects=True, vmem_limit_bytes=48 * 1024 * 1024
        ),
    )(features, weight, cotangent, tile_val, tile_row, tile_col, tile_count)
    lanes = pieces // 2
    weight_grad = (
        wgrad.reshape(2, lanes, 2, piece_rows, TILE).transpose(2, 3, 0, 1, 4).reshape(panel, hid).astype(F32)
    )
    high = panel - TILE
    right = jnp.concatenate([fgrad[2 * TILE :, :high], fgrad[2 * TILE :, high:]], axis=0)
    feature_grad = jnp.concatenate([fgrad[: 2 * TILE], right], axis=1)
    return hidden, weight_grad, feature_grad


def solution(mesh):
    placed = (
        P("blk", "rep"),
        P(),
        P("blk", "rep"),
        P("blk", None, None, None),
        P("blk", None),
        P("blk", None),
        P("blk"),
    )
    return jax.shard_map(
        body,
        mesh=mesh,
        in_specs=placed,
        out_specs=(P("blk", "rep"), P("rep", None), P("blk", "rep")),
        check_vma=False,
    )
```

```python
import functools

import jax
import jax.numpy as jnp
from jax import lax
from jax.experimental import pallas as pl
from jax.experimental.pallas import tpu as pltpu
from jax.sharding import PartitionSpec as P

TILE = 128
ROWT = 2
REACH = 4
WIDE = 2 * REACH + 1
ZL, NY, NX, NC = 2, 8, 8, 2
SUB = 16
VMEM_BYTES = 60 * 1024 * 1024
F32 = jnp.float32
BF16 = jnp.bfloat16


def mm(a, b):
    return jnp.dot(a, b, preferred_element_type=F32)


def mm_nt(a, b):
    return lax.dot_general(a, b, (((1,), (1,)), ((), ())), preferred_element_type=F32)


def remote(src, dst, send, recv, where):
    return pltpu.make_async_remote_copy(
        src_ref=src, dst_ref=dst, send_sem=send, recv_sem=recv,
        device_id=where, device_id_type=pl.DeviceIdType.MESH,
    )


def kernel(
    nodes, slots, reps,
    feat_hbm, weight_hbm, cot_hbm, val_hbm, row_hbm, col_hbm, count_hbm,
    hidden_out, wgrad_out, fgrad_out,
    row_ref, col_ref, count_ref,
    weight, vals, win, chain, adj, scale, acc,
    aggbuf, pre, cotbuf, grad, hidden, back, own_part, parts, backbuf, fgrad,
    core_out, core_in, core_own, y_out, y_in, x_out, x_in, xg, yg,
    local_sem, halo_s, halo_r, pass_s, pass_r, cot_s, cot_r, agg_s, agg_r, core_s, core_r,
    y_s, y_r, x_s, x_r, xg_s, xg_r, yg_s, yg_r, cg_s, cg_r, hb_s, hb_r, out_sem,
):
    blk = lax.axis_index("blk")
    rep = lax.axis_index("rep")
    blocks = ZL * NY * NX * NC
    core = blk % NC
    x = (blk // NC) % NX
    y = (blk // (NC * NX)) % NY
    zl = blk // (NC * NX * NY)
    xz = zl * NX + x
    toward = 1 - 2 * core
    panel = win.shape[1]
    pieces, piece_rows, _ = core_out.shape
    x_rows = x_out.shape[1]

    def blk_at(offset):
        return {"blk": (blk + offset + blocks) % blocks}

    def y_at(step):
        return {"blk": ((zl * NY + (y + step) % NY) * NX + x) * NC + core}

    def x_at(step):
        return {"blk": ((zl * NY + y) * NX + (x + step) % NX) * NC + core}

    def xz_at(step):
        g = (xz + step) % (ZL * NX)
        return {"blk": (((g // NX) * NY + y) * NX + g % NX) * NC + core}

    def rep_at(step):
        return {"rep": (rep + step) % reps}

    sibling = {"blk": blk + toward}
    offsets = [d for d in range(-REACH, REACH + 1) if d != 0]

    get_feat = pltpu.make_async_copy(feat_hbm, win.at[REACH], local_sem.at[0])
    get_feat.start()
    get_cot = pltpu.make_async_copy(cot_hbm, cotbuf.at[rep], local_sem.at[1])
    get_cot.start()

    barrier = pltpu.get_barrier_semaphore()

    def greet(where):
        pl.semaphore_signal(barrier, inc=1, device_id=where, device_id_type=pl.DeviceIdType.MESH)

    for d in offsets:
        greet(blk_at(d))
    for step in range(1, reps):
        greet(rep_at(step))
    for step in range(1, NY):
        greet(y_at(step))
    for step in range(1, ZL * NX):
        greet(xz_at(step))
    greeted = len(offsets) + reps - 1 + NY - 1 + ZL * NX - 1

    get_rows = pltpu.make_async_copy(row_hbm, row_ref, local_sem.at[2])
    get_cols = pltpu.make_async_copy(col_hbm, col_ref, local_sem.at[3])
    get_count = pltpu.make_async_copy(count_hbm, count_ref, local_sem.at[4])
    get_vals = pltpu.make_async_copy(val_hbm.at[0], vals, local_sem.at[5])
    get_weight = pltpu.make_async_copy(weight_hbm, weight, local_sem.at[6])
    for copy in (get_rows, get_cols, get_count, get_vals, get_weight):
        copy.start()
    get_feat.wait()
    get_cot.wait()
    get_rows.wait()
    get_cols.wait()
    get_count.wait()

    count = count_ref[0]
    keys = [jnp.where(s < count, row_ref[0, s] * (WIDE * ROWT) + col_ref[0, s], -1 - s) for s in range(slots)]
    rows = [jnp.where(s < count, row_ref[0, s], -1) for s in range(slots)]
    chain[slots] = jnp.zeros((TILE, TILE), F32)

    pl.semaphore_wait(barrier, greeted)

    halo = {}
    for i, d in enumerate((-4 * toward, 2, -2, 4 * toward)):
        halo[i] = remote(win.at[REACH], win.at[REACH - d], halo_s.at[i], halo_r.at[i], blk_at(d))
        halo[i].start()
    to_sibling = [remote(win.at[REACH], win.at[REACH - toward], pass_s.at[3], pass_r.at[3], sibling)]
    to_sibling[0].start()
    cots = []

    def gather_rep(buf, send, recv, out):
        for i, step in enumerate((1, -1) if reps > 2 else (1,)):
            copy = remote(buf.at[rep], buf.at[rep], send.at[i], recv.at[i], rep_at(step + reps))
            copy.start()
            out.append(copy)

    def pass_rep(buf, send, recv, out):
        half = buf.shape[1] // 2
        for i, step in enumerate((1, -1)):
            out[i].wait_recv()
            owner = (rep - step + reps) % reps
            at = buf.at[owner, pl.ds(i * half, half)]
            copy = remote(at, at, send.at[2 + i], recv.at[2 + i], rep_at(step + reps))
            copy.start()
            out.append(copy)

    gather_rep(cotbuf, cot_s, cot_r, cots)

    get_vals.wait()
    chunk = 32

    def one_where(cond):
        return jnp.where(cond, 1.0, 0.0).astype(F32)

    for s in range(slots):
        before = jnp.int32(slots)
        for t in range(s):
            before = jnp.where(keys[t] == keys[s], t, before)
        v = vals[s].astype(F32)
        chain[s] = v + chain[before]

    @pl.loop(0, TILE // chunk)
    def _(c):
        at = pl.ds(pl.multiple_of(c * chunk, chunk), chunk)
        sums = [jnp.zeros((chunk, TILE), F32) for _ in range(ROWT)]
        for s in range(slots):
            v = vals[s, at, :].astype(F32)
            sq = v * v
            for r in range(ROWT):
                sums[r] = sums[r] + sq * one_where(rows[s] == r)
        for r in range(ROWT):
            acc[pl.ds(pl.multiple_of(c * chunk, chunk), chunk), r * TILE : (r + 1) * TILE] = sums[r]

    for r in range(ROWT):
        row_sq = jnp.sum(acc[0:TILE, r * TILE : (r + 1) * TILE].T, axis=0, keepdims=True)
        scale[:, r * TILE : (r + 1) * TILE] = jnp.broadcast_to(lax.rsqrt(1.0 + row_sq), (8, TILE))

    @pl.loop(0, WIDE)
    def _(j):
        for r in range(ROWT):
            for t in range(ROWT):
                last = jnp.int32(slots)
                for s in range(slots):
                    last = jnp.where(keys[s] == r * (WIDE * ROWT) + j * ROWT + t, s, last)
                adj[j, r * TILE : (r + 1) * TILE, t * TILE : (t + 1) * TILE] = chain[last].astype(BF16)

    acc[...] = mm_nt(win[REACH], adj[REACH])

    def add_block(j):
        acc[...] += mm_nt(win[j], adj[j])

    for i, d in enumerate((-4 * toward, 2, -2)):
        halo[i].wait_recv()
        copy = remote(win.at[REACH - d], win.at[REACH - d - toward], pass_s.at[i], pass_r.at[i], sibling)
        copy.start()
        to_sibling.append(copy)
    if reps > 2:
        pass_rep(cotbuf, cot_s, cot_r, cots)
    halo[3].wait_recv()
    for d in (-4, -2, 2, 4):
        add_block(REACH + d)
    for copy in to_sibling:
        copy.wait_recv()
    for d in (-3, -1, 1, 3):
        add_block(REACH + d)

    node_scale = scale[0:1, :]
    aggbuf[rep] = (win[REACH].astype(F32) + node_scale * acc[...]).astype(BF16)
    aggs = []
    gather_rep(aggbuf, agg_s, agg_r, aggs)

    get_weight.wait()
    groups = pre.shape[0]
    wide = pre.shape[2]

    def weight_rows(q):
        return pl.ds(pl.multiple_of(q * panel, 64), panel)

    def add_pre(q, first):
        lhs = aggbuf[q].astype(F32).T.astype(BF16)
        for n in range(groups):
            part = mm(lhs, weight[weight_rows(q), n * wide : (n + 1) * wide])
            if first:
                pre[n] = part
            else:
                pre[n] += part

    add_pre(rep, True)
    if reps > 2:
        pass_rep(aggbuf, agg_s, agg_r, aggs)
        add_pre((rep + reps - 1) % reps, False)
        add_pre((rep + 1) % reps, False)
        for copy in cots[2:] + aggs[2:]:
            copy.wait_recv()
        add_pre((rep + 2) % reps, False)
    else:
        cots[0].wait_recv()
        aggs[0].wait_recv()
        add_pre((rep + 1) % reps, False)

    def grad_at(n):
        v = pre[n]
        sig = jax.nn.sigmoid(v)
        slope = sig * (1.0 + v * (1.0 - sig))
        grad[n] = (cotbuf[n].astype(F32) * slope).astype(BF16)

    def weight_part(n, u, out):
        part = mm(aggbuf[rep], grad[n]).astype(out.dtype)
        for t in range(wide // TILE):
            for h in range(2):
                out[(u * (wide // TILE) + t) * 2 + h] = part[
                    h * piece_rows : (h + 1) * piece_rows, t * TILE : (t + 1) * TILE
                ]

    half = groups // 2
    for u in range(half):
        n = (1 - core) * half + u
        grad_at(n)
        weight_part(n, u, core_out)
    core_copy = remote(core_out, core_in, core_s.at[0], core_r.at[0], sibling)
    core_copy.start()
    for u in range(half):
        n = core * half + u
        grad_at(n)
        weight_part(n, u, core_own)

    back_sum = mm_nt(weight[weight_rows(rep), 0:wide], grad[0])
    for n in range(1, groups):
        back_sum = back_sum + mm_nt(weight[weight_rows(rep), n * wide : (n + 1) * wide], grad[n])
    back[...] = back_sum

    core_copy.wait_recv()
    for i in range(pieces):
        total = core_own[i] + core_in[i].astype(F32)
        core_own[i] = total
        y_out[i] = total.astype(BF16)
    ys = []
    for step in (4, 3, 5, 2, 6, 1, 7) if NY == 8 else range(1, NY):
        copy = remote(y_out.at[(y + step) % NY], y_in.at[y], y_s.at[step], y_r.at[step], y_at(step))
        copy.start()
        ys.append(copy)

    scaled = (node_scale * back[...]).astype(BF16)
    hbs = []
    for d in (4, -4, 3, -3, 2, -2, 1, -1):
        j = REACH + d
        parts[j] = mm(scaled, adj[j]).astype(BF16)
        copy = remote(parts.at[j], backbuf.at[REACH - d], hb_s.at[d + REACH], hb_r.at[REACH - d], blk_at(d))
        copy.start()
        hbs.append(copy)
    own_part[...] = mm(scaled, adj[REACH]) + back[...]

    v = pre[rep]
    hidden[...] = (v * jax.nn.sigmoid(v)).astype(BF16)
    put_hidden = pltpu.make_async_copy(hidden, hidden_out, out_sem.at[0])
    put_hidden.start()

    for copy in ys:
        copy.wait_recv()
    total = core_own[y]
    for step in range(1, NY):
        total = total + y_in[(y + step) % NY].astype(F32)
    filled = piece_rows // x_rows
    x_out[0:filled] = total.astype(BF16).reshape(filled, x_rows, TILE)
    if filled < NX:
        x_out[filled:NX] = jnp.zeros((NX - filled, x_rows, TILE), BF16)
    xs = []
    for step in range(1, ZL * NX):
        to = ((xz + step) % (ZL * NX)) % NX
        copy = remote(x_out.at[to], x_in.at[xz], x_s.at[step], x_r.at[step], xz_at(step))
        copy.start()
        xs.append(copy)
    x_in[xz] = x_out[x]
    for copy in xs:
        copy.wait_recv()
    total = x_in[0].astype(F32)
    for g in range(1, ZL * NX):
        total = total + x_in[g].astype(F32)
    xg[x] = (total * nodes ** -0.5).astype(BF16)
    xgs = []
    for step in range(1, NX):
        copy = remote(xg.at[x], xg.at[x], xg_s.at[step], xg_r.at[step], x_at(step))
        copy.start()
        xgs.append(copy)
    for copy in xgs:
        copy.wait_recv()
    yg[y] = xg[0:filled].reshape(piece_rows, TILE)
    ygs = []
    for step in (4, 3, 5, 2, 6, 1, 7) if NY == 8 else range(1, NY):
        copy = remote(yg.at[y], yg.at[y], yg_s.at[step], yg_r.at[step], y_at(step))
        copy.start()
        ygs.append((step, copy))
    cgs = []
    puts = []

    def place(i):
        lane = core * (pieces // 2 * TILE) + (i // 2) * TILE
        at = (
            pl.ds(pl.multiple_of((i % 2) * piece_rows, piece_rows), piece_rows),
            pl.ds(pl.multiple_of(lane, TILE), TILE),
        )
        return wgrad_out.at[at]

    def pass_on(at, step):
        copy = remote(yg.at[at], place(at), cg_s.at[step], cg_r.at[step], sibling)
        copy.start()
        cgs.append(copy)
        copy = pltpu.make_async_copy(yg.at[at], place(at), out_sem.at[2 + step])
        copy.start()
        puts.append(copy)

    pass_on(y, 0)

    for copy in hbs:
        copy.wait_recv()
    total = own_part[...]
    for d in offsets:
        total = total + backbuf[REACH + d].astype(F32)
    fgrad[...] = total.astype(BF16)
    put_fgrad = pltpu.make_async_copy(fgrad, fgrad_out, out_sem.at[1])
    put_fgrad.start()

    for step, copy in sorted(ygs, key=lambda pair: min(pair[0], NY - pair[0])):
        copy.wait_recv()
        pass_on((y + NY - step) % NY, step)
    for copy in cgs + puts:
        copy.wait()
    put_hidden.wait()
    put_fgrad.wait()
    for copy in list(halo.values()) + to_sibling + cots + aggs + [core_copy] + ys + hbs + xs + xgs:
        copy.wait_send()
    for _, copy in ygs:
        copy.wait_send()


def finish(hidden_in, wgrad_in, fgrad_in, hidden_out, wgrad_out, fgrad_out, sems):
    put_hidden = pltpu.make_async_copy(hidden_in, hidden_out, sems.at[0])
    put_hidden.start()
    put_fgrad = pltpu.make_async_copy(fgrad_in, fgrad_out, sems.at[1])
    put_fgrad.start()
    wgrad_out[...] = wgrad_in[...].astype(F32)
    put_hidden.wait()
    put_fgrad.wait()


def body(features, weight, cotangent, tile_val, tile_row, tile_col, tile_count):
    rows, panel = features.shape
    slots = tile_val.shape[1]
    reps = lax.axis_size("rep")
    nodes = rows * lax.axis_size("blk")
    f_in, hid = weight.shape
    wide = cotangent.shape[1]
    pieces = hid // TILE
    piece_rows = panel // 2
    x_rows = SUB * (-(-piece_rows // (SUB * NX)))
    group = ZL * NX
    vmem = pltpu.VMEM
    smem = pltpu.SMEM
    dma = pltpu.SemaphoreType.DMA
    scratch = [
        smem((1, slots), jnp.int32),
        smem((1, slots), jnp.int32),
        smem((1,), jnp.int32),
        vmem((f_in, hid), BF16),
        vmem((slots, TILE, TILE), BF16),
        vmem((WIDE, panel, rows), BF16),
        vmem((slots + 1, TILE, TILE), F32),
        vmem((WIDE, rows, rows), BF16),
        vmem((8, rows), F32),
        vmem((panel, rows), F32),
        vmem((reps, panel, rows), BF16),
        vmem((reps, rows, wide), F32),
        vmem((reps, rows, wide), BF16),
        vmem((reps, rows, wide), BF16),
        vmem((rows, wide), BF16),
        vmem((panel, rows), F32),
        vmem((panel, rows), F32),
        vmem((WIDE, panel, rows), BF16),
        vmem((WIDE, panel, rows), BF16),
        vmem((panel, rows), BF16),
        vmem((pieces, piece_rows, TILE), BF16),
        vmem((pieces, piece_rows, TILE), BF16),
        vmem((pieces, piece_rows, TILE), F32),
        vmem((pieces, piece_rows, TILE), BF16),
        vmem((pieces, piece_rows, TILE), BF16),
        vmem((NX, x_rows, TILE), BF16),
        vmem((group, x_rows, TILE), BF16),
        vmem((NX, x_rows, TILE), BF16),
        vmem((pieces, piece_rows, TILE), BF16),
    ] + [
        dma((n,))
        for n in (
            7, 4, 4, 4, 4, 4, 4, 4, 4, 1, 1,
            NY, NY, group, group, NX, NX, NY, NY, NY, NY, WIDE, WIDE, 2 + NY,
        )
    ]
    anywhere = pl.BlockSpec(memory_space=pl.ANY)
    hbm = pl.BlockSpec(memory_space=pltpu.HBM)
    whole = pl.BlockSpec(memory_space=pltpu.VMEM)
    results = pl.pallas_call(
        functools.partial(kernel, nodes, slots, reps),
        out_shape=(
            jax.ShapeDtypeStruct((rows, wide), BF16),
            jax.ShapeDtypeStruct((panel, hid), BF16),
            jax.ShapeDtypeStruct((panel, rows), BF16),
        ),
        in_specs=[hbm] * 7,
        out_specs=(anywhere,) * 3,
        scratch_shapes=scratch,
        compiler_params=pltpu.CompilerParams(
            collective_id=0, has_side_effects=True, vmem_limit_bytes=VMEM_BYTES
        ),
    )(features.T, weight, cotangent, tile_val, tile_row, tile_col, tile_count)
    hidden, weight_grad, feature_grad = pl.pallas_call(
        finish,
        out_shape=(
            jax.ShapeDtypeStruct((rows, wide), BF16),
            jax.ShapeDtypeStruct((panel, hid), F32),
            jax.ShapeDtypeStruct((panel, rows), BF16),
        ),
        in_specs=[anywhere, whole, anywhere],
        out_specs=(hbm, whole, hbm),
        scratch_shapes=[dma((2,))],
        compiler_params=pltpu.CompilerParams(vmem_limit_bytes=VMEM_BYTES),
    )(*results)
    return hidden, weight_grad, feature_grad.T


def solution(mesh):
    placed = (
        P("blk", "rep"),
        P(),
        P("blk", "rep"),
        P("blk", None, None, None),
        P("blk", None),
        P("blk", None),
        P("blk"),
    )
    return jax.shard_map(
        body,
        mesh=mesh,
        in_specs=placed,
        out_specs=(P("blk", "rep"), P("rep", None), P("blk", "rep")),
        check_vma=False,
    )
```

```python
import functools

import jax
import jax.numpy as jnp
from jax import lax
from jax.experimental import pallas as pl
from jax.experimental.pallas import tpu as pltpu
from jax.sharding import PartitionSpec as P

TILE = 128
ROWT = 2
REACH = 4
WIDE = 2 * REACH + 1
ZL, NY, NX, NC = 2, 8, 8, 2
SUB = 16
VMEM_BYTES = 60 * 1024 * 1024
F32 = jnp.float32
BF16 = jnp.bfloat16


def mm(a, b):
    return jnp.dot(a, b, preferred_element_type=F32)


def mm_nt(a, b):
    return lax.dot_general(a, b, (((1,), (1,)), ((), ())), preferred_element_type=F32)


def remote(src, dst, send, recv, where):
    return pltpu.make_async_remote_copy(
        src_ref=src, dst_ref=dst, send_sem=send, recv_sem=recv,
        device_id=where, device_id_type=pl.DeviceIdType.MESH,
    )


def kernel(
    nodes, slots, reps,
    feat_hbm, weight_hbm, cot_hbm, val_hbm, row_hbm, col_hbm, count_hbm,
    hidden_out, wgrad_out, fgrad_out,
    row_ref, col_ref, count_ref,
    weight, vals, win, chain, adj, scale, acc,
    aggbuf, pre, cotbuf, grad, hidden, back, own_part, parts, sibbuf, backbuf, fgrad,
    core_out, core_in, core_own, y_out, y_in, x_out, x_in, xg, yg,
    local_sem, halo_s, halo_r, pass_s, pass_r, cot_s, cot_r, agg_s, agg_r, core_s, core_r,
    y_s, y_r, x_s, x_r, xg_s, xg_r, yg_s, yg_r, cg_s, cg_r, hs_s, hs_r, hb_s, hb_r, out_sem,
):
    blk = lax.axis_index("blk")
    rep = lax.axis_index("rep")
    blocks = ZL * NY * NX * NC
    core = blk % NC
    x = (blk // NC) % NX
    y = (blk // (NC * NX)) % NY
    zl = blk // (NC * NX * NY)
    xz = zl * NX + x
    toward = 1 - 2 * core
    panel = win.shape[1]
    pieces, piece_rows, _ = core_out.shape
    x_rows = x_out.shape[1]

    def blk_at(offset):
        return {"blk": (blk + offset + blocks) % blocks}

    def y_at(step):
        return {"blk": ((zl * NY + (y + step) % NY) * NX + x) * NC + core}

    def x_at(step):
        return {"blk": ((zl * NY + y) * NX + (x + step) % NX) * NC + core}

    def xz_at(step):
        g = (xz + step) % (ZL * NX)
        return {"blk": (((g // NX) * NY + y) * NX + g % NX) * NC + core}

    def rep_at(step):
        return {"rep": (rep + step) % reps}

    sibling = {"blk": blk + toward}
    greet_at = [blk_at(d) for d in (-4, -2, 2, 4)] + [sibling]

    get_feat = pltpu.make_async_copy(feat_hbm, win.at[REACH], local_sem.at[0])
    get_feat.start()
    get_cot = pltpu.make_async_copy(cot_hbm, cotbuf.at[rep], local_sem.at[1])
    get_cot.start()

    barrier = pltpu.get_barrier_semaphore()

    def greet(where):
        pl.semaphore_signal(barrier, inc=1, device_id=where, device_id_type=pl.DeviceIdType.MESH)

    for where in greet_at:
        greet(where)
    for step in range(1, reps):
        greet(rep_at(step))
    for step in range(1, NY):
        greet(y_at(step))
    for step in range(1, ZL * NX):
        greet(xz_at(step))
    greeted = len(greet_at) + reps - 1 + NY - 1 + ZL * NX - 1

    get_rows = pltpu.make_async_copy(row_hbm, row_ref, local_sem.at[2])
    get_cols = pltpu.make_async_copy(col_hbm, col_ref, local_sem.at[3])
    get_count = pltpu.make_async_copy(count_hbm, count_ref, local_sem.at[4])
    get_vals = pltpu.make_async_copy(val_hbm.at[0], vals, local_sem.at[5])
    get_weight = pltpu.make_async_copy(weight_hbm, weight, local_sem.at[6])
    for copy in (get_rows, get_cols, get_count, get_vals, get_weight):
        copy.start()
    get_feat.wait()
    get_cot.wait()
    get_rows.wait()
    get_cols.wait()
    get_count.wait()

    count = count_ref[0]
    keys = [jnp.where(s < count, row_ref[0, s] * (WIDE * ROWT) + col_ref[0, s], -1 - s) for s in range(slots)]
    rows = [jnp.where(s < count, row_ref[0, s], -1) for s in range(slots)]
    chain[slots] = jnp.zeros((TILE, TILE), F32)

    pl.semaphore_wait(barrier, greeted)

    rows_half = panel // 2
    parts_of = [pl.ds(h * rows_half, rows_half) for h in range(2)]
    near = (-4 * toward, 2, -2, 4 * toward)
    halo = [[], []]
    to_sibling = [[], []]
    for h in range(2):
        own = win.at[REACH, parts_of[h]]
        for i, d in enumerate(near):
            copy = remote(own, win.at[REACH - d, parts_of[h]], halo_s.at[4 * h + i], halo_r.at[4 * h + i], blk_at(d))
            copy.start()
            halo[h].append(copy)
        copy = remote(own, win.at[REACH - toward, parts_of[h]], pass_s.at[4 * h + 3], pass_r.at[4 * h + 3], sibling)
        copy.start()
        to_sibling[h].append(copy)

    cots = []
    for i, step in enumerate((1, -1)):
        copy = remote(cotbuf.at[rep], cotbuf.at[rep], cot_s.at[i], cot_r.at[i], rep_at(step + reps))
        copy.start()
        cots.append(copy)

    get_vals.wait()
    chunk = 32

    def one_where(cond):
        return jnp.where(cond, 1.0, 0.0).astype(F32)

    for s in range(slots):
        before = jnp.int32(slots)
        for t in range(s):
            before = jnp.where(keys[t] == keys[s], t, before)
        v = vals[s].astype(F32)
        chain[s] = v + chain[before]

    @pl.loop(0, TILE // chunk)
    def _(c):
        at = pl.ds(pl.multiple_of(c * chunk, chunk), chunk)
        sums = [jnp.zeros((chunk, TILE), F32) for _ in range(ROWT)]
        for s in range(slots):
            v = vals[s, at, :].astype(F32)
            sq = v * v
            for r in range(ROWT):
                sums[r] = sums[r] + sq * one_where(rows[s] == r)
        for r in range(ROWT):
            acc[pl.ds(pl.multiple_of(c * chunk, chunk), chunk), r * TILE : (r + 1) * TILE] = sums[r]

    for r in range(ROWT):
        row_sq = jnp.sum(acc[0:TILE, r * TILE : (r + 1) * TILE].T, axis=0, keepdims=True)
        scale[:, r * TILE : (r + 1) * TILE] = jnp.broadcast_to(lax.rsqrt(1.0 + row_sq), (8, TILE))

    @pl.loop(0, WIDE)
    def _(j):
        for r in range(ROWT):
            for t in range(ROWT):
                last = jnp.int32(slots)
                for s in range(slots):
                    last = jnp.where(keys[s] == r * (WIDE * ROWT) + j * ROWT + t, s, last)
                adj[j, r * TILE : (r + 1) * TILE, t * TILE : (t + 1) * TILE] = chain[last].astype(BF16)

    node_scale = scale[0:1, :]
    aggs = [[], []]
    for h in range(2):
        total = mm_nt(win[REACH, parts_of[h], :], adj[REACH])
        for i, d in enumerate(near[:3]):
            halo[h][i].wait_recv()
            copy = remote(
                win.at[REACH - d, parts_of[h]], win.at[REACH - d - toward, parts_of[h]],
                pass_s.at[4 * h + i], pass_r.at[4 * h + i], sibling,
            )
            copy.start()
            to_sibling[h].append(copy)
        halo[h][3].wait_recv()
        for d in (-4, -2, 2, 4):
            total = total + mm_nt(win[REACH + d, parts_of[h], :], adj[REACH + d])
        for copy in to_sibling[h]:
            copy.wait_recv()
        for d in (-3, -1, 1, 3):
            total = total + mm_nt(win[REACH + d, parts_of[h], :], adj[REACH + d])
        aggbuf[rep, parts_of[h], :] = (win[REACH, parts_of[h], :].astype(F32) + node_scale * total).astype(BF16)
        for i, step in enumerate((1, -1)):
            at = aggbuf.at[rep, parts_of[h]]
            copy = remote(at, at, agg_s.at[2 * h + i], agg_r.at[2 * h + i], rep_at(step + reps))
            copy.start()
            aggs[h].append(copy)
        if h == 0:
            half = cotbuf.shape[1] // 2
            for i, step in enumerate((1, -1)):
                cots[i].wait_recv()
                at = cotbuf.at[(rep - step + reps) % reps, pl.ds(i * half, half)]
                copy = remote(at, at, cot_s.at[2 + i], cot_r.at[2 + i], rep_at(step + reps))
                copy.start()
                cots.append(copy)

    relays = []

    def relay(i, step):
        aggs[i][i].wait_recv()
        at = aggbuf.at[(rep - step + reps) % reps, parts_of[i]]
        copy = remote(at, at, agg_s.at[4 + i], agg_r.at[4 + i], rep_at(step + reps))
        copy.start()
        relays.append(copy)

    relay(0, 1)
    get_weight.wait()
    groups = pre.shape[0]
    wide = pre.shape[2]

    def weight_rows(q):
        return pl.ds(pl.multiple_of(q * panel, 64), panel)

    def add_pre(q, first):
        lhs = aggbuf[q].astype(F32).T.astype(BF16)
        for n in range(groups):
            part = mm(lhs, weight[weight_rows(q), n * wide : (n + 1) * wide])
            if first:
                pre[n] = part
            else:
                pre[n] += part

    add_pre(rep, True)
    relay(1, -1)
    aggs[1][0].wait_recv()
    add_pre((rep + reps - 1) % reps, False)
    aggs[0][1].wait_recv()
    add_pre((rep + 1) % reps, False)
    for copy in cots[2:] + relays:
        copy.wait_recv()
    add_pre((rep + 2) % reps, False)

    def grad_at(n):
        v = pre[n]
        sig = jax.nn.sigmoid(v)
        slope = sig * (1.0 + v * (1.0 - sig))
        grad[n] = (cotbuf[n].astype(F32) * slope).astype(BF16)

    def weight_part(n, u, out):
        part = mm(aggbuf[rep], grad[n]).astype(out.dtype)
        for t in range(wide // TILE):
            for h in range(2):
                out[(u * (wide // TILE) + t) * 2 + h] = part[
                    h * piece_rows : (h + 1) * piece_rows, t * TILE : (t + 1) * TILE
                ]

    half = groups // 2
    for u in range(half):
        n = (1 - core) * half + u
        grad_at(n)
        weight_part(n, u, core_out)
    core_copy = remote(core_out, core_in, core_s.at[0], core_r.at[0], sibling)
    core_copy.start()
    for u in range(half):
        n = core * half + u
        grad_at(n)
        weight_part(n, u, core_own)

    back_sum = mm_nt(weight[weight_rows(rep), 0:wide], grad[0])
    for n in range(1, groups):
        back_sum = back_sum + mm_nt(weight[weight_rows(rep), n * wide : (n + 1) * wide], grad[n])
    back[...] = back_sum

    core_copy.wait_recv()
    for i in range(pieces):
        total = core_own[i] + core_in[i].astype(F32)
        core_own[i] = total
        y_out[i] = total.astype(BF16)
    ys = []
    for step in (4, 3, 5, 2, 6, 1, 7) if NY == 8 else range(1, NY):
        copy = remote(y_out.at[(y + step) % NY], y_in.at[y], y_s.at[step], y_r.at[step], y_at(step))
        copy.start()
        ys.append(copy)

    scaled = (node_scale * back[...]).astype(BF16)
    hbs = []
    hss = []
    for i, d in enumerate((2, -2, -4 * toward)):
        j = REACH + d + toward
        parts[j] = mm(scaled, adj[j]).astype(BF16)
        copy = remote(parts.at[j], sibbuf.at[i], hs_s.at[i], hs_r.at[i], sibling)
        copy.start()
        hss.append(copy)

    def send_back(i, d, where):
        copy = remote(parts.at[REACH + d], backbuf.at[i], hb_s.at[i], hb_r.at[i], where)
        copy.start()
        hbs.append(copy)

    for i, d, where in ((3, -4 * toward, blk_at(-4 * toward)), (4, toward, sibling)):
        parts[REACH + d] = mm(scaled, adj[REACH + d]).astype(BF16)
        send_back(i, d, where)
    for i, d in enumerate((2, -2, 4 * toward)):
        mine = mm(scaled, adj[REACH + d])
        hss[i].wait_recv()
        parts[REACH + d] = (mine + sibbuf[i].astype(F32)).astype(BF16)
        send_back(i, d, blk_at(d))
    own_part[...] = mm(scaled, adj[REACH]) + back[...]

    v = pre[rep]
    hidden[...] = (v * jax.nn.sigmoid(v)).astype(BF16)
    put_hidden = pltpu.make_async_copy(hidden, hidden_out, out_sem.at[0])
    put_hidden.start()

    for copy in ys:
        copy.wait_recv()
    total = core_own[y]
    for step in range(1, NY):
        total = total + y_in[(y + step) % NY].astype(F32)
    filled = piece_rows // x_rows
    x_out[0:filled] = total.astype(BF16).reshape(filled, x_rows, TILE)
    if filled < NX:
        x_out[filled:NX] = jnp.zeros((NX - filled, x_rows, TILE), BF16)
    xs = []
    for step in range(1, ZL * NX):
        to = ((xz + step) % (ZL * NX)) % NX
        copy = remote(x_out.at[to], x_in.at[xz], x_s.at[step], x_r.at[step], xz_at(step))
        copy.start()
        xs.append(copy)
    x_in[xz] = x_out[x]
    for copy in xs:
        copy.wait_recv()
    total = x_in[0].astype(F32)
    for g in range(1, ZL * NX):
        total = total + x_in[g].astype(F32)
    xg[x] = (total * nodes ** -0.5).astype(BF16)
    xgs = []
    for step in range(1, NX):
        copy = remote(xg.at[x], xg.at[x], xg_s.at[step], xg_r.at[step], x_at(step))
        copy.start()
        xgs.append(copy)
    for copy in xgs:
        copy.wait_recv()
    yg[y] = xg[0:filled].reshape(piece_rows, TILE)
    ygs = []
    for step in (4, 3, 5, 2, 6, 1, 7) if NY == 8 else range(1, NY):
        copy = remote(yg.at[y], yg.at[y], yg_s.at[step], yg_r.at[step], y_at(step))
        copy.start()
        ygs.append((step, copy))
    cgs = []
    puts = []

    def place(i):
        lane = core * (pieces // 2 * TILE) + (i // 2) * TILE
        at = (
            pl.ds(pl.multiple_of((i % 2) * piece_rows, piece_rows), piece_rows),
            pl.ds(pl.multiple_of(lane, TILE), TILE),
        )
        return wgrad_out.at[at]

    def pass_on(at, step):
        copy = remote(yg.at[at], place(at), cg_s.at[step], cg_r.at[step], sibling)
        copy.start()
        cgs.append(copy)
        copy = pltpu.make_async_copy(yg.at[at], place(at), out_sem.at[2 + step])
        copy.start()
        puts.append(copy)

    pass_on(y, 0)

    for copy in hbs:
        copy.wait_recv()
    total = own_part[...]
    for i in range(5):
        total = total + backbuf[i].astype(F32)
    fgrad[...] = total.astype(BF16)
    put_fgrad = pltpu.make_async_copy(fgrad, fgrad_out, out_sem.at[1])
    put_fgrad.start()

    for step, copy in sorted(ygs, key=lambda pair: min(pair[0], NY - pair[0])):
        copy.wait_recv()
        pass_on((y + NY - step) % NY, step)
    for copy in cgs + puts:
        copy.wait()
    put_hidden.wait()
    put_fgrad.wait()
    gathers = halo[0] + halo[1] + to_sibling[0] + to_sibling[1] + cots + aggs[0] + aggs[1] + relays
    for copy in gathers + [core_copy] + ys + hss + hbs + xs + xgs:
        copy.wait_send()
    for _, copy in ygs:
        copy.wait_send()


def finish(hidden_in, wgrad_in, fgrad_in, hidden_out, wgrad_out, fgrad_out):
    hidden_out[...] = hidden_in[...]
    fgrad_out[...] = fgrad_in[...]
    wgrad_out[...] = wgrad_in[...].astype(F32)


def body(features, weight, cotangent, tile_val, tile_row, tile_col, tile_count):
    rows, panel = features.shape
    slots = tile_val.shape[1]
    reps = lax.axis_size("rep")
    nodes = rows * lax.axis_size("blk")
    f_in, hid = weight.shape
    wide = cotangent.shape[1]
    pieces = hid // TILE
    piece_rows = panel // 2
    x_rows = SUB * (-(-piece_rows // (SUB * NX)))
    group = ZL * NX
    vmem = pltpu.VMEM
    smem = pltpu.SMEM
    dma = pltpu.SemaphoreType.DMA
    scratch = [
        smem((1, slots), jnp.int32),
        smem((1, slots), jnp.int32),
        smem((1,), jnp.int32),
        vmem((f_in, hid), BF16),
        vmem((slots, TILE, TILE), BF16),
        vmem((WIDE, panel, rows), BF16),
        vmem((slots + 1, TILE, TILE), F32),
        vmem((WIDE, rows, rows), BF16),
        vmem((8, rows), F32),
        vmem((TILE, rows), F32),
        vmem((reps, panel, rows), BF16),
        vmem((reps, rows, wide), F32),
        vmem((reps, rows, wide), BF16),
        vmem((reps, rows, wide), BF16),
        vmem((rows, wide), BF16),
        vmem((panel, rows), F32),
        vmem((panel, rows), F32),
        vmem((WIDE, panel, rows), BF16),
        vmem((3, panel, rows), BF16),
        vmem((5, panel, rows), BF16),
        vmem((panel, rows), BF16),
        vmem((pieces, piece_rows, TILE), BF16),
        vmem((pieces, piece_rows, TILE), BF16),
        vmem((pieces, piece_rows, TILE), F32),
        vmem((pieces, piece_rows, TILE), BF16),
        vmem((pieces, piece_rows, TILE), BF16),
        vmem((NX, x_rows, TILE), BF16),
        vmem((group, x_rows, TILE), BF16),
        vmem((NX, x_rows, TILE), BF16),
        vmem((pieces, piece_rows, TILE), BF16),
    ] + [
        dma((n,))
        for n in (
            7, 8, 8, 8, 8, 4, 4, 6, 6, 1, 1,
            NY, NY, group, group, NX, NX, NY, NY, NY, NY, 3, 3, 5, 5, 2 + NY,
        )
    ]
    anywhere = pl.BlockSpec(memory_space=pl.ANY)
    hbm = pl.BlockSpec(memory_space=pltpu.HBM)
    whole = pl.BlockSpec(memory_space=pltpu.VMEM)
    results = pl.pallas_call(
        functools.partial(kernel, nodes, slots, reps),
        out_shape=(
            jax.ShapeDtypeStruct((rows, wide), BF16),
            jax.ShapeDtypeStruct((panel, hid), BF16),
            jax.ShapeDtypeStruct((panel, rows), BF16),
        ),
        in_specs=[hbm] * 7,
        out_specs=(anywhere,) * 3,
        scratch_shapes=scratch,
        compiler_params=pltpu.CompilerParams(
            collective_id=0, has_side_effects=True, vmem_limit_bytes=VMEM_BYTES
        ),
    )(features.T, weight, cotangent, tile_val, tile_row, tile_col, tile_count)
    hidden, weight_grad, feature_grad = pl.pallas_call(
        finish,
        out_shape=(
            jax.ShapeDtypeStruct((rows, wide), BF16),
            jax.ShapeDtypeStruct((panel, hid), F32),
            jax.ShapeDtypeStruct((panel, rows), BF16),
        ),
        in_specs=[whole] * 3,
        out_specs=(whole,) * 3,
        compiler_params=pltpu.CompilerParams(vmem_limit_bytes=VMEM_BYTES),
    )(*results)
    return hidden, weight_grad, feature_grad.T


def solution(mesh):
    placed = (
        P("blk", "rep"),
        P(),
        P("blk", "rep"),
        P("blk", None, None, None),
        P("blk", None),
        P("blk", None),
        P("blk"),
    )
    return jax.shard_map(
        body,
        mesh=mesh,
        in_specs=placed,
        out_specs=(P("blk", "rep"), P("rep", None), P("blk", "rep")),
        check_vma=False,
    )
```

```python
import functools

import jax
import jax.numpy as jnp
from jax import lax
from jax.experimental import pallas as pl
from jax.experimental.pallas import tpu as pltpu
from jax.sharding import PartitionSpec as P

TILE = 128
ROWT = 2
REACH = 4
WIDE = 2 * REACH + 1
ZL, NY, NX, NC = 2, 8, 8, 2
SUB = 16
VMEM_BYTES = 60 * 1024 * 1024
F32 = jnp.float32
BF16 = jnp.bfloat16


def mm(a, b):
    return jnp.dot(a, b, preferred_element_type=F32)


def mm_nt(a, b):
    return lax.dot_general(a, b, (((1,), (1,)), ((), ())), preferred_element_type=F32)


def remote(src, dst, send, recv, where):
    return pltpu.make_async_remote_copy(
        src_ref=src, dst_ref=dst, send_sem=send, recv_sem=recv,
        device_id=where, device_id_type=pl.DeviceIdType.MESH,
    )


def kernel(
    nodes, slots, reps,
    feat_hbm, weight_hbm, cot_hbm, val_hbm, row_hbm, col_hbm, count_hbm,
    hidden_out, wgrad_out, fgrad_out,
    row_ref, col_ref, count_ref,
    weight, vals, win, chain, adj, scale, acc,
    aggbuf, pre, cotbuf, grad, hidden, back, own_part, parts, sibbuf, outbuf, backbuf, fgrad,
    core_out, core_in, core_own, y_out, y_in, x_out, x_in, xg, yg,
    local_sem, halo_s, halo_r, pass_s, pass_r, cot_s, cot_r, agg_s, agg_r, core_s, core_r,
    y_s, y_r, x_s, x_r, xg_s, xg_r, yg_s, yg_r, cg_s, cg_r, hs_s, hs_r, hb_s, hb_r, out_sem,
):
    blk = lax.axis_index("blk")
    rep = lax.axis_index("rep")
    blocks = ZL * NY * NX * NC
    core = blk % NC
    x = (blk // NC) % NX
    y = (blk // (NC * NX)) % NY
    zl = blk // (NC * NX * NY)
    xz = zl * NX + x
    toward = 1 - 2 * core
    panel = win.shape[1]
    pieces, piece_rows, _ = core_out.shape
    x_rows = x_out.shape[1]

    def blk_at(offset):
        return {"blk": (blk + offset + blocks) % blocks}

    def y_at(step):
        return {"blk": ((zl * NY + (y + step) % NY) * NX + x) * NC + core}

    def x_at(step):
        return {"blk": ((zl * NY + y) * NX + (x + step) % NX) * NC + core}

    def xz_at(step):
        g = (xz + step) % (ZL * NX)
        return {"blk": (((g // NX) * NY + y) * NX + g % NX) * NC + core}

    def rep_at(step):
        return {"rep": (rep + step) % reps}

    sibling = {"blk": blk + toward}
    greet_at = [blk_at(d) for d in (-4, -2, 2, 4)] + [sibling]

    get_feat = pltpu.make_async_copy(feat_hbm, win.at[REACH], local_sem.at[0])
    get_feat.start()
    get_cot = pltpu.make_async_copy(cot_hbm, cotbuf.at[rep], local_sem.at[1])
    get_cot.start()

    barrier = pltpu.get_barrier_semaphore()

    def greet(where):
        pl.semaphore_signal(barrier, inc=1, device_id=where, device_id_type=pl.DeviceIdType.MESH)

    for where in greet_at:
        greet(where)
    for step in (1, -1):
        greet(rep_at(step + reps))
    for step in range(1, NY):
        greet(y_at(step))
    for step in range(1, ZL * NX):
        greet(xz_at(step))
    greeted = len(greet_at) + 2 + NY - 1 + ZL * NX - 1

    get_rows = pltpu.make_async_copy(row_hbm, row_ref, local_sem.at[2])
    get_cols = pltpu.make_async_copy(col_hbm, col_ref, local_sem.at[3])
    get_count = pltpu.make_async_copy(count_hbm, count_ref, local_sem.at[4])
    get_vals = pltpu.make_async_copy(val_hbm.at[0], vals, local_sem.at[5])
    get_weight = pltpu.make_async_copy(weight_hbm, weight, local_sem.at[6])
    for copy in (get_rows, get_cols, get_count, get_vals, get_weight):
        copy.start()
    get_feat.wait()
    get_cot.wait()
    get_rows.wait()
    get_cols.wait()
    get_count.wait()

    count = count_ref[0]
    keys = [jnp.where(s < count, row_ref[0, s] * (WIDE * ROWT) + col_ref[0, s], -1 - s) for s in range(slots)]
    rows = [jnp.where(s < count, row_ref[0, s], -1) for s in range(slots)]
    chain[slots] = jnp.zeros((TILE, TILE), F32)

    pl.semaphore_wait(barrier, greeted)

    rows_half = panel // 2
    parts_of = [pl.ds(h * rows_half, rows_half) for h in range(2)]
    near = (-4 * toward, 2, -2, 4 * toward)
    halo = [[], []]
    to_sibling = [[], []]
    for h in range(2):
        own = win.at[REACH, parts_of[h]]
        for i, d in enumerate(near):
            copy = remote(own, win.at[REACH - d, parts_of[h]], halo_s.at[4 * h + i], halo_r.at[4 * h + i], blk_at(d))
            copy.start()
            halo[h].append(copy)
        copy = remote(own, win.at[REACH - toward, parts_of[h]], pass_s.at[4 * h + 3], pass_r.at[4 * h + 3], sibling)
        copy.start()
        to_sibling[h].append(copy)

    cots = []
    for i, step in enumerate((1, -1)):
        copy = remote(cotbuf.at[rep], cotbuf.at[rep], cot_s.at[i], cot_r.at[i], rep_at(step + reps))
        copy.start()
        cots.append(copy)

    get_vals.wait()
    chunk = 32

    def one_where(cond):
        return jnp.where(cond, 1.0, 0.0).astype(F32)

    for s in range(slots):
        before = jnp.int32(slots)
        for t in range(s):
            before = jnp.where(keys[t] == keys[s], t, before)
        v = vals[s].astype(F32)
        chain[s] = v + chain[before]

    @pl.loop(0, TILE // chunk)
    def _(c):
        at = pl.ds(pl.multiple_of(c * chunk, chunk), chunk)
        sums = [jnp.zeros((chunk, TILE), F32) for _ in range(ROWT)]
        for s in range(slots):
            v = vals[s, at, :].astype(F32)
            sq = v * v
            for r in range(ROWT):
                sums[r] = sums[r] + sq * one_where(rows[s] == r)
        for r in range(ROWT):
            acc[pl.ds(pl.multiple_of(c * chunk, chunk), chunk), r * TILE : (r + 1) * TILE] = sums[r]

    for r in range(ROWT):
        row_sq = jnp.sum(acc[0:TILE, r * TILE : (r + 1) * TILE].T, axis=0, keepdims=True)
        scale[:, r * TILE : (r + 1) * TILE] = jnp.broadcast_to(lax.rsqrt(1.0 + row_sq), (8, TILE))

    @pl.loop(0, WIDE)
    def _(j):
        for r in range(ROWT):
            for t in range(ROWT):
                last = jnp.int32(slots)
                for s in range(slots):
                    last = jnp.where(keys[s] == r * (WIDE * ROWT) + j * ROWT + t, s, last)
                adj[j, r * TILE : (r + 1) * TILE, t * TILE : (t + 1) * TILE] = chain[last].astype(BF16)

    node_scale = scale[0:1, :]
    aggs = [[], []]
    for h in range(2):
        total = mm_nt(win[REACH, parts_of[h], :], adj[REACH])
        for i, d in enumerate(near[:3]):
            halo[h][i].wait_recv()
            copy = remote(
                win.at[REACH - d, parts_of[h]], win.at[REACH - d - toward, parts_of[h]],
                pass_s.at[4 * h + i], pass_r.at[4 * h + i], sibling,
            )
            copy.start()
            to_sibling[h].append(copy)
        halo[h][3].wait_recv()
        for d in (-4, -2, 2, 4):
            total = total + mm_nt(win[REACH + d, parts_of[h], :], adj[REACH + d])
        for copy in to_sibling[h]:
            copy.wait_recv()
        for d in (-3, -1, 1, 3):
            total = total + mm_nt(win[REACH + d, parts_of[h], :], adj[REACH + d])
        aggbuf[rep, parts_of[h], :] = (win[REACH, parts_of[h], :].astype(F32) + node_scale * total).astype(BF16)
        for i, step in enumerate((1, -1)):
            at = aggbuf.at[rep, parts_of[h]]
            copy = remote(at, at, agg_s.at[2 * h + i], agg_r.at[2 * h + i], rep_at(step + reps))
            copy.start()
            aggs[h].append(copy)
        if h == 0:
            half = cotbuf.shape[1] // 2
            for i, step in enumerate((1, -1)):
                cots[i].wait_recv()
                at = cotbuf.at[(rep - step + reps) % reps, pl.ds(i * half, half)]
                copy = remote(at, at, cot_s.at[2 + i], cot_r.at[2 + i], rep_at(step + reps))
                copy.start()
                cots.append(copy)

    relays = []

    def relay(i, step):
        aggs[i][i].wait_recv()
        at = aggbuf.at[(rep - step + reps) % reps, parts_of[i]]
        copy = remote(at, at, agg_s.at[4 + i], agg_r.at[4 + i], rep_at(step + reps))
        copy.start()
        relays.append(copy)

    relay(0, 1)
    get_weight.wait()
    groups = pre.shape[0]
    wide = pre.shape[2]

    def weight_rows(q):
        return pl.ds(pl.multiple_of(q * panel, 64), panel)

    def add_pre(q, first):
        lhs = aggbuf[q].astype(F32).T.astype(BF16)
        for n in range(groups):
            part = mm(lhs, weight[weight_rows(q), n * wide : (n + 1) * wide])
            if first:
                pre[n] = part
            else:
                pre[n] += part

    add_pre(rep, True)
    relay(1, -1)
    aggs[1][0].wait_recv()
    add_pre((rep + reps - 1) % reps, False)
    aggs[0][1].wait_recv()
    add_pre((rep + 1) % reps, False)
    for copy in cots[2:] + relays:
        copy.wait_recv()
    add_pre((rep + 2) % reps, False)

    def grad_at(n):
        v = pre[n]
        sig = jax.nn.sigmoid(v)
        slope = sig * (1.0 + v * (1.0 - sig))
        grad[n] = (cotbuf[n].astype(F32) * slope).astype(BF16)

    def weight_part(n, u, out):
        part = mm(aggbuf[rep], grad[n]).astype(out.dtype)
        for t in range(wide // TILE):
            for h in range(2):
                out[(u * (wide // TILE) + t) * 2 + h] = part[
                    h * piece_rows : (h + 1) * piece_rows, t * TILE : (t + 1) * TILE
                ]

    half = groups // 2
    share = pieces // half
    core_copies = []
    for u in range(half):
        n = (1 - core) * half + u
        grad_at(n)
        weight_part(n, u, core_out)
        at = pl.ds(u * share, share)
        copy = remote(core_out.at[at], core_in.at[at], core_s.at[u], core_r.at[u], sibling)
        copy.start()
        core_copies.append(copy)
    for u in range(half):
        n = core * half + u
        grad_at(n)
        weight_part(n, u, core_own)

    def to_y(i):
        where = {"blk": ((zl * NY + i) * NX + x) * NC + core}
        return remote(y_out.at[i], y_in.at[y], y_s.at[i], y_r.at[y], where)

    for u in range(half):
        core_copies[u].wait_recv()
        for i in range(u * share, (u + 1) * share):
            total = core_own[i] + core_in[i].astype(F32)
            core_own[i] = total
            y_out[i] = total.astype(BF16)

            @pl.when(y != i)
            def _(i=i):
                to_y(i).start()

    back_sum = mm_nt(weight[weight_rows(rep), 0:wide], grad[0])
    for n in range(1, groups):
        back_sum = back_sum + mm_nt(weight[weight_rows(rep), n * wide : (n + 1) * wide], grad[n])
    back[...] = back_sum

    scaled = (node_scale * back[...]).astype(BF16)
    hss = []
    for i, d in enumerate((2, -2, -4 * toward)):
        j = REACH + d + toward
        parts[i] = mm(scaled, adj[j]).astype(BF16)
        copy = remote(parts.at[i], sibbuf.at[i], hs_s.at[i], hs_r.at[i], sibling)
        copy.start()
        hss.append(copy)

    hb_list = ((3, -4 * toward), (4, toward), (0, 2), (1, -2), (2, 4 * toward))
    for i, d in hb_list:
        mine = mm(scaled, adj[REACH + d])
        if i < 3:
            hss[i].wait_recv()
            mine = mine + sibbuf[i].astype(F32)
        outbuf[i] = mine.astype(BF16)
    own_part[...] = mm(scaled, adj[REACH]) + back[...]

    v = pre[rep]
    hidden[...] = (v * jax.nn.sigmoid(v)).astype(BF16)
    put_hidden = pltpu.make_async_copy(hidden, hidden_out, out_sem.at[0])
    put_hidden.start()

    total = core_own[y]
    for step in range(1, NY):
        source = (y + step) % NY
        remote(y_out.at[source], y_in.at[source], y_s.at[source], y_r.at[source], y_at(step)).wait_recv()
    for step in range(1, NY):
        total = total + y_in[(y + step) % NY].astype(F32)
    filled = piece_rows // x_rows
    x_out[0:filled] = total.astype(BF16).reshape(filled, x_rows, TILE)
    if filled < NX:
        x_out[filled:NX] = jnp.zeros((NX - filled, x_rows, TILE), BF16)
    xs = []
    for step in range(1, ZL * NX):
        to = ((xz + step) % (ZL * NX)) % NX
        copy = remote(x_out.at[to], x_in.at[xz], x_s.at[step], x_r.at[step], xz_at(step))
        copy.start()
        xs.append(copy)
    x_in[xz] = x_out[x]
    for copy in xs:
        copy.wait_recv()
    total = x_in[0].astype(F32)
    for g in range(1, ZL * NX):
        total = total + x_in[g].astype(F32)
    xg[x] = (total * nodes ** -0.5).astype(BF16)
    xgs = []
    for step in range(1, NX):
        copy = remote(xg.at[x], xg.at[x], xg_s.at[step], xg_r.at[step], x_at(step))
        copy.start()
        xgs.append(copy)
    hbs = []
    for i, d in hb_list:
        copy = remote(outbuf.at[i], backbuf.at[i], hb_s.at[i], hb_r.at[i], sibling if i == 4 else blk_at(d))
        copy.start()
        hbs.append(copy)
    for copy in xgs:
        copy.wait_recv()
    yg[y] = xg[0:filled].reshape(piece_rows, TILE)
    ygs = []
    for step in (4, 3, 5, 2, 6, 1, 7) if NY == 8 else range(1, NY):
        copy = remote(yg.at[y], yg.at[y], yg_s.at[step], yg_r.at[step], y_at(step))
        copy.start()
        ygs.append((step, copy))
    cgs = []
    puts = []

    def place(i):
        lane = core * (pieces // 2 * TILE) + (i // 2) * TILE
        at = (
            pl.ds(pl.multiple_of((i % 2) * piece_rows, piece_rows), piece_rows),
            pl.ds(pl.multiple_of(lane, TILE), TILE),
        )
        return wgrad_out.at[at]

    def pass_on(at, step):
        copy = remote(yg.at[at], place(at), cg_s.at[step], cg_r.at[step], sibling)
        copy.start()
        cgs.append(copy)
        copy = pltpu.make_async_copy(yg.at[at], place(at), out_sem.at[2 + step])
        copy.start()
        puts.append(copy)

    pass_on(y, 0)

    for step, copy in sorted(ygs, key=lambda pair: min(pair[0], NY - pair[0])):
        copy.wait_recv()
        pass_on((y + NY - step) % NY, step)

    for copy in hbs:
        copy.wait_recv()
    total = own_part[...]
    for i in range(5):
        total = total + backbuf[i].astype(F32)
    fgrad[...] = total.astype(BF16)
    put_fgrad = pltpu.make_async_copy(fgrad, fgrad_out, out_sem.at[1])
    put_fgrad.start()

    for copy in cgs + puts:
        copy.wait()
    put_hidden.wait()
    put_fgrad.wait()
    gathers = halo[0] + halo[1] + to_sibling[0] + to_sibling[1] + cots + aggs[0] + aggs[1] + relays
    for i in range(NY):

        @pl.when(y != i)
        def _(i=i):
            to_y(i).wait_send()

    for copy in gathers + core_copies + hss + hbs + xs + xgs:
        copy.wait_send()
    for _, copy in ygs:
        copy.wait_send()


def finish(hidden_in, wgrad_in, fgrad_in, hidden_out, wgrad_out, fgrad_out):
    hidden_out[...] = hidden_in[...]
    fgrad_out[...] = fgrad_in[...]
    wgrad_out[...] = wgrad_in[...].astype(F32)


def body(features, weight, cotangent, tile_val, tile_row, tile_col, tile_count):
    rows, panel = features.shape
    slots = tile_val.shape[1]
    reps = lax.axis_size("rep")
    nodes = rows * lax.axis_size("blk")
    f_in, hid = weight.shape
    wide = cotangent.shape[1]
    pieces = hid // TILE
    piece_rows = panel // 2
    x_rows = SUB * (-(-piece_rows // (SUB * NX)))
    group = ZL * NX
    vmem = pltpu.VMEM
    smem = pltpu.SMEM
    dma = pltpu.SemaphoreType.DMA
    scratch = [
        smem((1, slots), jnp.int32),
        smem((1, slots), jnp.int32),
        smem((1,), jnp.int32),
        vmem((f_in, hid), BF16),
        vmem((slots, TILE, TILE), BF16),
        vmem((WIDE, panel, rows), BF16),
        vmem((slots + 1, TILE, TILE), F32),
        vmem((WIDE, rows, rows), BF16),
        vmem((8, rows), F32),
        vmem((TILE, rows), F32),
        vmem((reps, panel, rows), BF16),
        vmem((reps, rows, wide), F32),
        vmem((reps, rows, wide), BF16),
        vmem((reps, rows, wide), BF16),
        vmem((rows, wide), BF16),
        vmem((panel, rows), F32),
        vmem((panel, rows), F32),
        vmem((3, panel, rows), BF16),
        vmem((3, panel, rows), BF16),
        vmem((5, panel, rows), BF16),
        vmem((5, panel, rows), BF16),
        vmem((panel, rows), BF16),
        vmem((pieces, piece_rows, TILE), BF16),
        vmem((pieces, piece_rows, TILE), BF16),
        vmem((pieces, piece_rows, TILE), F32),
        vmem((pieces, piece_rows, TILE), BF16),
        vmem((pieces, piece_rows, TILE), BF16),
        vmem((NX, x_rows, TILE), BF16),
        vmem((group, x_rows, TILE), BF16),
        vmem((NX, x_rows, TILE), BF16),
        vmem((pieces, piece_rows, TILE), BF16),
    ] + [
        dma((n,))
        for n in (
            7, 8, 8, 8, 8, 4, 4, 6, 6, 2, 2,
            NY, NY, group, group, NX, NX, NY, NY, NY, NY, 3, 3, 5, 5, 2 + NY,
        )
    ]
    anywhere = pl.BlockSpec(memory_space=pl.ANY)
    hbm = pl.BlockSpec(memory_space=pltpu.HBM)
    whole = pl.BlockSpec(memory_space=pltpu.VMEM)
    results = pl.pallas_call(
        functools.partial(kernel, nodes, slots, reps),
        out_shape=(
            jax.ShapeDtypeStruct((rows, wide), BF16),
            jax.ShapeDtypeStruct((panel, hid), BF16),
            jax.ShapeDtypeStruct((panel, rows), BF16),
        ),
        in_specs=[hbm] * 7,
        out_specs=(anywhere,) * 3,
        scratch_shapes=scratch,
        compiler_params=pltpu.CompilerParams(
            collective_id=0, has_side_effects=True, vmem_limit_bytes=VMEM_BYTES
        ),
    )(features.T, weight, cotangent, tile_val, tile_row, tile_col, tile_count)
    hidden, weight_grad, feature_grad = pl.pallas_call(
        finish,
        out_shape=(
            jax.ShapeDtypeStruct((rows, wide), BF16),
            jax.ShapeDtypeStruct((panel, hid), F32),
            jax.ShapeDtypeStruct((panel, rows), BF16),
        ),
        in_specs=[whole] * 3,
        out_specs=(whole,) * 3,
        compiler_params=pltpu.CompilerParams(vmem_limit_bytes=VMEM_BYTES),
    )(*results)
    return hidden, weight_grad, feature_grad.T


def solution(mesh):
    placed = (
        P("blk", "rep"),
        P(),
        P("blk", "rep"),
        P("blk", None, None, None),
        P("blk", None),
        P("blk", None),
        P("blk"),
    )
    return jax.shard_map(
        body,
        mesh=mesh,
        in_specs=placed,
        out_specs=(P("blk", "rep"), P("rep", None), P("blk", "rep")),
        check_vma=False,
    )
```

```python
import functools

import jax
import jax.numpy as jnp
from jax import lax
from jax.experimental import pallas as pl
from jax.experimental.pallas import tpu as pltpu
from jax.sharding import PartitionSpec as P

TILE = 128
ROWT = 2
REACH = 4
WIDE = 2 * REACH + 1
ZL, NY, NX, NC = 2, 8, 8, 2
SUB = 16
VMEM_BYTES = 60 * 1024 * 1024
F32 = jnp.float32
BF16 = jnp.bfloat16


def mm(a, b):
    return jnp.dot(a, b, preferred_element_type=F32)


def mm_nt(a, b):
    return lax.dot_general(a, b, (((1,), (1,)), ((), ())), preferred_element_type=F32)


def remote(src, dst, send, recv, where):
    return pltpu.make_async_remote_copy(
        src_ref=src, dst_ref=dst, send_sem=send, recv_sem=recv,
        device_id=where, device_id_type=pl.DeviceIdType.MESH,
    )


def kernel(
    nodes, slots, reps,
    feat_hbm, weight_hbm, cot_hbm, val_hbm, row_hbm, col_hbm, count_hbm,
    hidden_out, wgrad_out, fgrad_out,
    row_ref, col_ref, count_ref,
    weight, vals, win, chain, adj, scale, acc,
    aggbuf, pre, cotbuf, grad, hidden, back, own_part, parts, sibbuf, outbuf, backbuf, fgrad,
    core_out, core_in, core_own, y_out, y_in, x_out, x_in, xg, yg,
    local_sem, halo_s, halo_r, pass_s, pass_r, cot_s, cot_r, agg_s, agg_r, core_s, core_r,
    y_s, y_r, x_s, x_r, xg_s, xg_r, yg_s, yg_r, cg_s, cg_r, hs_s, hs_r, hb_s, hb_r, out_sem,
):
    blk = lax.axis_index("blk")
    rep = lax.axis_index("rep")
    blocks = ZL * NY * NX * NC
    core = blk % NC
    x = (blk // NC) % NX
    y = (blk // (NC * NX)) % NY
    zl = blk // (NC * NX * NY)
    xz = zl * NX + x
    toward = 1 - 2 * core
    panel = win.shape[1]
    pieces, piece_rows, _ = core_out.shape
    x_rows = x_out.shape[1]

    def blk_at(offset):
        return {"blk": (blk + offset + blocks) % blocks}

    def y_at(step):
        return {"blk": ((zl * NY + (y + step) % NY) * NX + x) * NC + core}

    def x_at(step):
        return {"blk": ((zl * NY + y) * NX + (x + step) % NX) * NC + core}

    def xz_at(step):
        g = (xz + step) % (ZL * NX)
        return {"blk": (((g // NX) * NY + y) * NX + g % NX) * NC + core}

    def rep_at(step):
        return {"rep": (rep + step) % reps}

    sibling = {"blk": blk + toward}
    greet_at = [blk_at(d) for d in (-4, -2, 2, 4)] + [sibling]

    get_feat = pltpu.make_async_copy(feat_hbm, win.at[REACH], local_sem.at[0])
    get_feat.start()
    get_cot = pltpu.make_async_copy(cot_hbm, cotbuf.at[rep], local_sem.at[1])
    get_cot.start()

    barrier = pltpu.get_barrier_semaphore()

    def greet(where):
        pl.semaphore_signal(barrier, inc=1, device_id=where, device_id_type=pl.DeviceIdType.MESH)

    for where in greet_at:
        greet(where)
    for step in (1, -1):
        greet(rep_at(step + reps))
    for step in range(1, NY):
        greet(y_at(step))
    for step in range(1, ZL * NX):
        greet(xz_at(step))
    greeted = len(greet_at) + 2 + NY - 1 + ZL * NX - 1

    get_rows = pltpu.make_async_copy(row_hbm, row_ref, local_sem.at[2])
    get_cols = pltpu.make_async_copy(col_hbm, col_ref, local_sem.at[3])
    get_count = pltpu.make_async_copy(count_hbm, count_ref, local_sem.at[4])
    get_vals = pltpu.make_async_copy(val_hbm.at[0], vals, local_sem.at[5])
    get_weight = pltpu.make_async_copy(weight_hbm, weight, local_sem.at[6])
    for copy in (get_rows, get_cols, get_count, get_vals, get_weight):
        copy.start()
    get_feat.wait()
    get_cot.wait()
    get_rows.wait()
    get_cols.wait()
    get_count.wait()

    count = count_ref[0]
    keys = [jnp.where(s < count, row_ref[0, s] * (WIDE * ROWT) + col_ref[0, s], -1 - s) for s in range(slots)]
    rows = [jnp.where(s < count, row_ref[0, s], -1) for s in range(slots)]
    chain[slots] = jnp.zeros((TILE, TILE), F32)

    pl.semaphore_wait(barrier, greeted)

    rows_half = panel // 2
    parts_of = [pl.ds(h * rows_half, rows_half) for h in range(2)]
    near = (-4 * toward, 2, -2, 4 * toward)
    halo = [[], []]
    to_sibling = [[], []]
    for h in range(2):
        own = win.at[REACH, parts_of[h]]
        for i, d in enumerate(near):
            copy = remote(own, win.at[REACH - d, parts_of[h]], halo_s.at[4 * h + i], halo_r.at[4 * h + i], blk_at(d))
            copy.start()
            halo[h].append(copy)
        copy = remote(own, win.at[REACH - toward, parts_of[h]], pass_s.at[4 * h + 3], pass_r.at[4 * h + 3], sibling)
        copy.start()
        to_sibling[h].append(copy)

    cots = []
    for i, step in enumerate((1, -1)):
        copy = remote(cotbuf.at[rep], cotbuf.at[rep], cot_s.at[i], cot_r.at[i], rep_at(step + reps))
        copy.start()
        cots.append(copy)

    get_vals.wait()
    chunk = 32

    def one_where(cond):
        return jnp.where(cond, 1.0, 0.0).astype(F32)

    for s in range(slots):
        before = jnp.int32(slots)
        for t in range(s):
            before = jnp.where(keys[t] == keys[s], t, before)
        v = vals[s].astype(F32)
        chain[s] = v + chain[before]

    @pl.loop(0, TILE // chunk)
    def _(c):
        at = pl.ds(pl.multiple_of(c * chunk, chunk), chunk)
        sums = [jnp.zeros((chunk, TILE), F32) for _ in range(ROWT)]
        for s in range(slots):
            v = vals[s, at, :].astype(F32)
            sq = v * v
            for r in range(ROWT):
                sums[r] = sums[r] + sq * one_where(rows[s] == r)
        for r in range(ROWT):
            acc[pl.ds(pl.multiple_of(c * chunk, chunk), chunk), r * TILE : (r + 1) * TILE] = sums[r]

    for r in range(ROWT):
        row_sq = jnp.sum(acc[0:TILE, r * TILE : (r + 1) * TILE].T, axis=0, keepdims=True)
        scale[:, r * TILE : (r + 1) * TILE] = jnp.broadcast_to(lax.rsqrt(1.0 + row_sq), (8, TILE))

    @pl.loop(0, WIDE)
    def _(j):
        for r in range(ROWT):
            for t in range(ROWT):
                last = jnp.int32(slots)
                for s in range(slots):
                    last = jnp.where(keys[s] == r * (WIDE * ROWT) + j * ROWT + t, s, last)
                adj[j, r * TILE : (r + 1) * TILE, t * TILE : (t + 1) * TILE] = chain[last].astype(BF16)

    node_scale = scale[0:1, :]
    aggs = [[], []]
    for h in range(2):
        total = mm_nt(win[REACH, parts_of[h], :], adj[REACH])
        for i in (1, 2, 0):
            d = near[i]
            halo[h][i].wait_recv()
            copy = remote(
                win.at[REACH - d, parts_of[h]], win.at[REACH - d - toward, parts_of[h]],
                pass_s.at[4 * h + i], pass_r.at[4 * h + i], sibling,
            )
            copy.start()
            to_sibling[h].append(copy)
        halo[h][3].wait_recv()
        for d in (-4, -2, 2, 4):
            total = total + mm_nt(win[REACH + d, parts_of[h], :], adj[REACH + d])
        for copy in to_sibling[h]:
            copy.wait_recv()
        for d in (-3, -1, 1, 3):
            total = total + mm_nt(win[REACH + d, parts_of[h], :], adj[REACH + d])
        aggbuf[rep, parts_of[h], :] = (win[REACH, parts_of[h], :].astype(F32) + node_scale * total).astype(BF16)
        for i, step in enumerate((1, -1)):
            at = aggbuf.at[rep, parts_of[h]]
            copy = remote(at, at, agg_s.at[2 * h + i], agg_r.at[2 * h + i], rep_at(step + reps))
            copy.start()
            aggs[h].append(copy)
        if h == 0:
            half = cotbuf.shape[1] // 2
            for i, step in enumerate((1, -1)):
                cots[i].wait_recv()
                at = cotbuf.at[(rep - step + reps) % reps, pl.ds(i * half, half)]
                copy = remote(at, at, cot_s.at[2 + i], cot_r.at[2 + i], rep_at(step + reps))
                copy.start()
                cots.append(copy)

    relays = []

    def relay(i, step):
        aggs[i][i].wait_recv()
        at = aggbuf.at[(rep - step + reps) % reps, parts_of[i]]
        copy = remote(at, at, agg_s.at[4 + i], agg_r.at[4 + i], rep_at(step + reps))
        copy.start()
        relays.append(copy)

    relay(0, 1)
    get_weight.wait()
    groups = pre.shape[0]
    wide = pre.shape[2]

    def weight_rows(q):
        return pl.ds(pl.multiple_of(q * panel, 64), panel)

    def add_pre(q, first):
        lhs = aggbuf[q].astype(F32).T.astype(BF16)
        for n in range(groups):
            part = mm(lhs, weight[weight_rows(q), n * wide : (n + 1) * wide])
            if first:
                pre[n] = part
            else:
                pre[n] += part

    add_pre(rep, True)
    relay(1, -1)
    aggs[1][0].wait_recv()
    add_pre((rep + reps - 1) % reps, False)
    aggs[0][1].wait_recv()
    add_pre((rep + 1) % reps, False)
    for copy in cots[2:] + relays:
        copy.wait_recv()
    last = (rep + 2) % reps
    last_lhs = aggbuf[last].astype(F32).T.astype(BF16)

    def grad_at(n):
        v = pre[n] + mm(last_lhs, weight[weight_rows(last), pl.ds(pl.multiple_of(n * wide, wide), wide)])
        pre[n] = v
        sig = jax.nn.sigmoid(v)
        slope = sig * (1.0 + v * (1.0 - sig))
        grad[n] = (cotbuf[n].astype(F32) * slope).astype(BF16)

    def weight_part(n, u, out):
        part = mm(aggbuf[rep], grad[n]).astype(out.dtype)
        for t in range(wide // TILE):
            for h in range(2):
                out[(u * (wide // TILE) + t) * 2 + h] = part[
                    h * piece_rows : (h + 1) * piece_rows, t * TILE : (t + 1) * TILE
                ]

    half = groups // 2
    share = pieces // half
    core_copies = []
    for u in range(half):
        n = (1 - core) * half + u
        grad_at(n)
        weight_part(n, u, core_out)
        at = pl.ds(u * share, share)
        copy = remote(core_out.at[at], core_in.at[at], core_s.at[u], core_r.at[u], sibling)
        copy.start()
        core_copies.append(copy)
    for u in range(half):
        n = core * half + u
        grad_at(n)
        weight_part(n, u, core_own)

    def to_y(i):
        where = {"blk": ((zl * NY + i) * NX + x) * NC + core}
        return remote(y_out.at[i], y_in.at[y], y_s.at[i], y_r.at[y], where)

    for u in range(half):
        core_copies[u].wait_recv()
        for i in range(u * share, (u + 1) * share):
            total = core_own[i] + core_in[i].astype(F32)
            core_own[i] = total
            y_out[i] = total.astype(BF16)

            @pl.when(y != i)
            def _(i=i):
                to_y(i).start()

    back_sum = mm_nt(weight[weight_rows(rep), 0:wide], grad[0])
    for n in range(1, groups):
        back_sum = back_sum + mm_nt(weight[weight_rows(rep), n * wide : (n + 1) * wide], grad[n])
    back[...] = back_sum

    scaled = (node_scale * back[...]).astype(BF16)
    hss = []
    for i, d in enumerate((2, -2, -4 * toward)):
        j = REACH + d + toward
        parts[i] = mm(scaled, adj[j]).astype(BF16)
        copy = remote(parts.at[i], sibbuf.at[i], hs_s.at[i], hs_r.at[i], sibling)
        copy.start()
        hss.append(copy)

    hb_list = ((3, -4 * toward), (4, toward), (0, 2), (1, -2), (2, 4 * toward))
    for i, d in hb_list:
        mine = mm(scaled, adj[REACH + d])
        if i < 3:
            hss[i].wait_recv()
            mine = mine + sibbuf[i].astype(F32)
        outbuf[i] = mine.astype(BF16)
    own_part[...] = mm(scaled, adj[REACH]) + back[...]

    v = pre[rep]
    hidden[...] = (v * jax.nn.sigmoid(v)).astype(BF16)
    put_hidden = pltpu.make_async_copy(hidden, hidden_out, out_sem.at[0])
    put_hidden.start()

    total = core_own[y]
    for step in range(1, NY):
        source = (y + step) % NY
        remote(y_out.at[source], y_in.at[source], y_s.at[source], y_r.at[source], y_at(step)).wait_recv()
    for step in range(1, NY):
        total = total + y_in[(y + step) % NY].astype(F32)
    filled = piece_rows // x_rows
    x_out[0:filled] = total.astype(BF16).reshape(filled, x_rows, TILE)
    if filled < NX:
        x_out[filled:NX] = jnp.zeros((NX - filled, x_rows, TILE), BF16)
    xs = []
    for step in range(1, ZL * NX):
        to = ((xz + step) % (ZL * NX)) % NX
        copy = remote(x_out.at[to], x_in.at[xz], x_s.at[step], x_r.at[step], xz_at(step))
        copy.start()
        xs.append(copy)
    x_in[xz] = x_out[x]
    hbs = []
    for i, d in hb_list:
        copy = remote(outbuf.at[i], backbuf.at[i], hb_s.at[i], hb_r.at[i], sibling if i == 4 else blk_at(d))
        copy.start()
        hbs.append(copy)
    for copy in xs:
        copy.wait_recv()
    total = x_in[0].astype(F32)
    for g in range(1, ZL * NX):
        total = total + x_in[g].astype(F32)
    xg[x] = (total * nodes ** -0.5).astype(BF16)
    xgs = []
    for step in range(1, NX):
        copy = remote(xg.at[x], xg.at[x], xg_s.at[step], xg_r.at[step], x_at(step))
        copy.start()
        xgs.append(copy)
    for copy in xgs:
        copy.wait_recv()
    yg[y] = xg[0:filled].reshape(piece_rows, TILE)
    ygs = []
    for step in (4, 3, 5, 2, 6, 1, 7) if NY == 8 else range(1, NY):
        copy = remote(yg.at[y], yg.at[y], yg_s.at[step], yg_r.at[step], y_at(step))
        copy.start()
        ygs.append((step, copy))
    cgs = []
    puts = []

    def place(i):
        lane = core * (pieces // 2 * TILE) + (i // 2) * TILE
        at = (
            pl.ds(pl.multiple_of((i % 2) * piece_rows, piece_rows), piece_rows),
            pl.ds(pl.multiple_of(lane, TILE), TILE),
        )
        return wgrad_out.at[at]

    def pass_on(at, step):
        copy = remote(yg.at[at], place(at), cg_s.at[step], cg_r.at[step], sibling)
        copy.start()
        cgs.append(copy)
        copy = pltpu.make_async_copy(yg.at[at], place(at), out_sem.at[2 + step])
        copy.start()
        puts.append(copy)

    pass_on(y, 0)

    for step, copy in sorted(ygs, key=lambda pair: min(pair[0], NY - pair[0])):
        copy.wait_recv()
        pass_on((y + NY - step) % NY, step)

    for copy in hbs:
        copy.wait_recv()
    total = own_part[...]
    for i in range(5):
        total = total + backbuf[i].astype(F32)
    fgrad[...] = total.astype(BF16)
    put_fgrad = pltpu.make_async_copy(fgrad, fgrad_out, out_sem.at[1])
    put_fgrad.start()

    for copy in cgs + puts:
        copy.wait()
    put_hidden.wait()
    put_fgrad.wait()
    gathers = halo[0] + halo[1] + to_sibling[0] + to_sibling[1] + cots + aggs[0] + aggs[1] + relays
    for i in range(NY):

        @pl.when(y != i)
        def _(i=i):
            to_y(i).wait_send()

    for copy in gathers + core_copies + hss + hbs + xs + xgs:
        copy.wait_send()
    for _, copy in ygs:
        copy.wait_send()


def finish(hidden_in, wgrad_in, fgrad_in, hidden_out, wgrad_out, fgrad_out):
    hidden_out[...] = hidden_in[...]
    fgrad_out[...] = fgrad_in[...]
    wgrad_out[...] = wgrad_in[...].astype(F32)


def body(features, weight, cotangent, tile_val, tile_row, tile_col, tile_count):
    rows, panel = features.shape
    slots = tile_val.shape[1]
    reps = lax.axis_size("rep")
    nodes = rows * lax.axis_size("blk")
    f_in, hid = weight.shape
    wide = cotangent.shape[1]
    pieces = hid // TILE
    piece_rows = panel // 2
    x_rows = SUB * (-(-piece_rows // (SUB * NX)))
    group = ZL * NX
    vmem = pltpu.VMEM
    smem = pltpu.SMEM
    dma = pltpu.SemaphoreType.DMA
    scratch = [
        smem((1, slots), jnp.int32),
        smem((1, slots), jnp.int32),
        smem((1,), jnp.int32),
        vmem((f_in, hid), BF16),
        vmem((slots, TILE, TILE), BF16),
        vmem((WIDE, panel, rows), BF16),
        vmem((slots + 1, TILE, TILE), F32),
        vmem((WIDE, rows, rows), BF16),
        vmem((8, rows), F32),
        vmem((TILE, rows), F32),
        vmem((reps, panel, rows), BF16),
        vmem((reps, rows, wide), F32),
        vmem((reps, rows, wide), BF16),
        vmem((reps, rows, wide), BF16),
        vmem((rows, wide), BF16),
        vmem((panel, rows), F32),
        vmem((panel, rows), F32),
        vmem((3, panel, rows), BF16),
        vmem((3, panel, rows), BF16),
        vmem((5, panel, rows), BF16),
        vmem((5, panel, rows), BF16),
        vmem((panel, rows), BF16),
        vmem((pieces, piece_rows, TILE), BF16),
        vmem((pieces, piece_rows, TILE), BF16),
        vmem((pieces, piece_rows, TILE), F32),
        vmem((pieces, piece_rows, TILE), BF16),
        vmem((pieces, piece_rows, TILE), BF16),
        vmem((NX, x_rows, TILE), BF16),
        vmem((group, x_rows, TILE), BF16),
        vmem((NX, x_rows, TILE), BF16),
        vmem((pieces, piece_rows, TILE), BF16),
    ] + [
        dma((n,))
        for n in (
            7, 8, 8, 8, 8, 4, 4, 6, 6, 2, 2,
            NY, NY, group, group, NX, NX, NY, NY, NY, NY, 3, 3, 5, 5, 2 + NY,
        )
    ]
    anywhere = pl.BlockSpec(memory_space=pl.ANY)
    hbm = pl.BlockSpec(memory_space=pltpu.HBM)
    whole = pl.BlockSpec(memory_space=pltpu.VMEM)
    results = pl.pallas_call(
        functools.partial(kernel, nodes, slots, reps),
        out_shape=(
            jax.ShapeDtypeStruct((rows, wide), BF16),
            jax.ShapeDtypeStruct((panel, hid), BF16),
            jax.ShapeDtypeStruct((panel, rows), BF16),
        ),
        in_specs=[hbm] * 7,
        out_specs=(anywhere,) * 3,
        scratch_shapes=scratch,
        compiler_params=pltpu.CompilerParams(
            collective_id=0, has_side_effects=True, vmem_limit_bytes=VMEM_BYTES
        ),
    )(features.T, weight, cotangent, tile_val, tile_row, tile_col, tile_count)
    hidden, weight_grad, feature_grad = pl.pallas_call(
        finish,
        out_shape=(
            jax.ShapeDtypeStruct((rows, wide), BF16),
            jax.ShapeDtypeStruct((panel, hid), F32),
            jax.ShapeDtypeStruct((panel, rows), BF16),
        ),
        in_specs=[whole] * 3,
        out_specs=(whole,) * 3,
        compiler_params=pltpu.CompilerParams(vmem_limit_bytes=VMEM_BYTES),
    )(*results)
    return hidden, weight_grad, feature_grad.T


def solution(mesh):
    placed = (
        P("blk", "rep"),
        P(),
        P("blk", "rep"),
        P("blk", None, None, None),
        P("blk", None),
        P("blk", None),
        P("blk"),
    )
    return jax.shard_map(
        body,
        mesh=mesh,
        in_specs=placed,
        out_specs=(P("blk", "rep"), P("rep", None), P("blk", "rep")),
        check_vma=False,
    )
```

```python
import functools

import jax
import jax.numpy as jnp
from jax import lax
from jax.experimental import pallas as pl
from jax.experimental.pallas import tpu as pltpu
from jax.sharding import PartitionSpec as P

TILE = 128
ROWT = 2
REACH = 4
WIDE = 2 * REACH + 1
ZL, NY, NX, NC = 2, 8, 8, 2
SUB = 16
VMEM_BYTES = 60 * 1024 * 1024
F32 = jnp.float32
BF16 = jnp.bfloat16


def mm(a, b):
    return jnp.dot(a, b, preferred_element_type=F32)


def mm_nt(a, b):
    return lax.dot_general(a, b, (((1,), (1,)), ((), ())), preferred_element_type=F32)


def remote(src, dst, send, recv, where):
    return pltpu.make_async_remote_copy(
        src_ref=src, dst_ref=dst, send_sem=send, recv_sem=recv,
        device_id=where, device_id_type=pl.DeviceIdType.MESH,
    )


def kernel(
    nodes, slots, reps,
    feat_hbm, weight_hbm, cot_hbm, val_hbm, row_hbm, col_hbm, count_hbm,
    hidden_out, wgrad_out, fgrad_out,
    row_ref, col_ref, count_ref,
    weight, vals, win, chain, adj, scale, acc,
    aggbuf, pre, cotbuf, grad, hidden, back, own_part, parts, sibbuf, outbuf, backbuf, fgrad,
    core_out, core_in, core_own, y_out, y_in, x_out, x_in, xg, yg,
    local_sem, halo_s, halo_r, pass_s, pass_r, cot_s, cot_r, agg_s, agg_r, core_s, core_r,
    y_s, y_r, x_s, x_r, xg_s, xg_r, yg_s, yg_r, cg_s, cg_r, hs_s, hs_r, hb_s, hb_r, out_sem,
):
    blk = lax.axis_index("blk")
    rep = lax.axis_index("rep")
    blocks = ZL * NY * NX * NC
    core = blk % NC
    x = (blk // NC) % NX
    y = (blk // (NC * NX)) % NY
    zl = blk // (NC * NX * NY)
    xz = zl * NX + x
    toward = 1 - 2 * core
    panel = win.shape[1]
    pieces, piece_rows, _ = core_out.shape
    x_rows = x_out.shape[1]

    def blk_at(offset):
        return {"blk": (blk + offset + blocks) % blocks}

    def y_at(step):
        return {"blk": ((zl * NY + (y + step) % NY) * NX + x) * NC + core}

    def x_at(step):
        return {"blk": ((zl * NY + y) * NX + (x + step) % NX) * NC + core}

    def xz_at(step):
        g = (xz + step) % (ZL * NX)
        return {"blk": (((g // NX) * NY + y) * NX + g % NX) * NC + core}

    def rep_at(step):
        return {"rep": (rep + step) % reps}

    sibling = {"blk": blk + toward}
    greet_at = [blk_at(d) for d in (-4, -2, 2, 4)] + [sibling]

    get_feat = pltpu.make_async_copy(feat_hbm, win.at[REACH], local_sem.at[0])
    get_feat.start()
    get_cot = pltpu.make_async_copy(cot_hbm, cotbuf.at[rep], local_sem.at[1])
    get_cot.start()

    barrier = pltpu.get_barrier_semaphore()

    def greet(where):
        pl.semaphore_signal(barrier, inc=1, device_id=where, device_id_type=pl.DeviceIdType.MESH)

    for where in greet_at:
        greet(where)
    for step in (1, -1):
        greet(rep_at(step + reps))
    for step in range(1, NY):
        greet(y_at(step))
    for step in range(1, ZL * NX):
        greet(xz_at(step))
    greeted = len(greet_at) + 2 + NY - 1 + ZL * NX - 1

    get_rows = pltpu.make_async_copy(row_hbm, row_ref, local_sem.at[2])
    get_cols = pltpu.make_async_copy(col_hbm, col_ref, local_sem.at[3])
    get_count = pltpu.make_async_copy(count_hbm, count_ref, local_sem.at[4])
    get_vals = pltpu.make_async_copy(val_hbm.at[0], vals, local_sem.at[5])
    get_weight = pltpu.make_async_copy(weight_hbm, weight, local_sem.at[6])
    for copy in (get_rows, get_cols, get_count, get_vals, get_weight):
        copy.start()
    get_feat.wait()
    get_cot.wait()
    get_rows.wait()
    get_cols.wait()
    get_count.wait()

    count = count_ref[0]
    keys = [jnp.where(s < count, row_ref[0, s] * (WIDE * ROWT) + col_ref[0, s], -1 - s) for s in range(slots)]
    rows = [jnp.where(s < count, row_ref[0, s], -1) for s in range(slots)]
    chain[slots] = jnp.zeros((TILE, TILE), F32)

    pl.semaphore_wait(barrier, greeted)

    rows_half = panel // 2
    parts_of = [pl.ds(h * rows_half, rows_half) for h in range(2)]
    near = (-4 * toward, 2, -2, 4 * toward)
    halo = [[], []]
    to_sibling = [[], []]
    for h in range(2):
        own = win.at[REACH, parts_of[h]]
        for i, d in enumerate(near):
            copy = remote(own, win.at[REACH - d, parts_of[h]], halo_s.at[4 * h + i], halo_r.at[4 * h + i], blk_at(d))
            copy.start()
            halo[h].append(copy)
        copy = remote(own, win.at[REACH - toward, parts_of[h]], pass_s.at[4 * h + 3], pass_r.at[4 * h + 3], sibling)
        copy.start()
        to_sibling[h].append(copy)

    cots = []
    for i, step in enumerate((1, -1)):
        copy = remote(cotbuf.at[rep], cotbuf.at[rep], cot_s.at[i], cot_r.at[i], rep_at(step + reps))
        copy.start()
        cots.append(copy)

    get_vals.wait()
    chunk = 32

    def one_where(cond):
        return jnp.where(cond, 1.0, 0.0).astype(F32)

    for s in range(slots):
        before = jnp.int32(slots)
        for t in range(s):
            before = jnp.where(keys[t] == keys[s], t, before)
        v = vals[s].astype(F32)
        chain[s] = v + chain[before]

    @pl.loop(0, TILE // chunk)
    def _(c):
        at = pl.ds(pl.multiple_of(c * chunk, chunk), chunk)
        sums = [jnp.zeros((chunk, TILE), F32) for _ in range(ROWT)]
        for s in range(slots):
            v = vals[s, at, :].astype(F32)
            sq = v * v
            for r in range(ROWT):
                sums[r] = sums[r] + sq * one_where(rows[s] == r)
        for r in range(ROWT):
            acc[pl.ds(pl.multiple_of(c * chunk, chunk), chunk), r * TILE : (r + 1) * TILE] = sums[r]

    for r in range(ROWT):
        row_sq = jnp.sum(acc[0:TILE, r * TILE : (r + 1) * TILE].T, axis=0, keepdims=True)
        scale[:, r * TILE : (r + 1) * TILE] = jnp.broadcast_to(lax.rsqrt(1.0 + row_sq), (8, TILE))

    @pl.loop(0, WIDE)
    def _(j):
        for r in range(ROWT):
            for t in range(ROWT):
                last = jnp.int32(slots)
                for s in range(slots):
                    last = jnp.where(keys[s] == r * (WIDE * ROWT) + j * ROWT + t, s, last)
                adj[j, r * TILE : (r + 1) * TILE, t * TILE : (t + 1) * TILE] = chain[last].astype(BF16)

    node_scale = scale[0:1, :]
    aggs = [[], []]
    for h in range(2):
        total = mm_nt(win[REACH, parts_of[h], :], adj[REACH])
        for i in (1, 2, 0):
            d = near[i]
            halo[h][i].wait_recv()
            copy = remote(
                win.at[REACH - d, parts_of[h]], win.at[REACH - d - toward, parts_of[h]],
                pass_s.at[4 * h + i], pass_r.at[4 * h + i], sibling,
            )
            copy.start()
            to_sibling[h].append(copy)
        halo[h][3].wait_recv()
        for d in (-4, -2, 2, 4):
            total = total + mm_nt(win[REACH + d, parts_of[h], :], adj[REACH + d])
        for copy in to_sibling[h]:
            copy.wait_recv()
        for d in (-3, -1, 1, 3):
            total = total + mm_nt(win[REACH + d, parts_of[h], :], adj[REACH + d])
        aggbuf[rep, parts_of[h], :] = (win[REACH, parts_of[h], :].astype(F32) + node_scale * total).astype(BF16)
        for i, step in enumerate((1, -1)):
            at = aggbuf.at[rep, parts_of[h]]
            copy = remote(at, at, agg_s.at[2 * h + i], agg_r.at[2 * h + i], rep_at(step + reps))
            copy.start()
            aggs[h].append(copy)
        if h == 0:
            half = cotbuf.shape[1] // 2
            for i, step in enumerate((1, -1)):
                cots[i].wait_recv()
                at = cotbuf.at[(rep - step + reps) % reps, pl.ds(i * half, half)]
                copy = remote(at, at, cot_s.at[2 + i], cot_r.at[2 + i], rep_at(step + reps))
                copy.start()
                cots.append(copy)

    relays = []

    def relay(i, step):
        aggs[i][i].wait_recv()
        at = aggbuf.at[(rep - step + reps) % reps, parts_of[i]]
        copy = remote(at, at, agg_s.at[4 + i], agg_r.at[4 + i], rep_at(step + reps))
        copy.start()
        relays.append(copy)

    relay(0, 1)
    get_weight.wait()
    groups = pre.shape[0]
    wide = pre.shape[2]

    def weight_rows(q):
        return pl.ds(pl.multiple_of(q * panel, 64), panel)

    def add_pre(q, first):
        lhs = aggbuf[q].astype(F32).T.astype(BF16)
        for n in range(groups):
            part = mm(lhs, weight[weight_rows(q), n * wide : (n + 1) * wide])
            if first:
                pre[n] = part
            else:
                pre[n] += part

    add_pre(rep, True)
    relay(1, -1)
    aggs[1][0].wait_recv()
    add_pre((rep + reps - 1) % reps, False)
    aggs[0][1].wait_recv()
    add_pre((rep + 1) % reps, False)
    for copy in cots[2:] + relays:
        copy.wait_recv()
    last = (rep + 2) % reps
    last_lhs = aggbuf[last].astype(F32).T.astype(BF16)

    def grad_at(n):
        v = pre[n] + mm(last_lhs, weight[weight_rows(last), pl.ds(pl.multiple_of(n * wide, wide), wide)])
        pre[n] = v
        sig = jax.nn.sigmoid(v)
        slope = sig * (1.0 + v * (1.0 - sig))
        grad[n] = (cotbuf[n].astype(F32) * slope).astype(BF16)

    def weight_part(n, u, out):
        part = mm(aggbuf[rep], grad[n]).astype(out.dtype)
        for t in range(wide // TILE):
            for h in range(2):
                out[(u * (wide // TILE) + t) * 2 + h] = part[
                    h * piece_rows : (h + 1) * piece_rows, t * TILE : (t + 1) * TILE
                ]

    half = groups // 2
    share = pieces // half
    core_copies = []
    for u in range(half):
        n = (1 - core) * half + u
        grad_at(n)
        weight_part(n, u, core_out)
        at = pl.ds(u * share, share)
        copy = remote(core_out.at[at], core_in.at[at], core_s.at[u], core_r.at[u], sibling)
        copy.start()
        core_copies.append(copy)
    for u in range(half):
        n = core * half + u
        grad_at(n)
        weight_part(n, u, core_own)

    for u in range(half):
        core_copies[u].wait_recv()
        for i in range(u * share, (u + 1) * share):
            total = core_own[i] + core_in[i].astype(F32)
            core_own[i] = total
            y_out[i] = total.astype(BF16)
    ys = []
    for step in (4, 3, 5, 2, 6, 1, 7) if NY == 8 else range(1, NY):
        copy = remote(y_out.at[(y + step) % NY], y_in.at[y], y_s.at[step], y_r.at[step], y_at(step))
        copy.start()
        ys.append(copy)

    back_sum = mm_nt(weight[weight_rows(rep), 0:wide], grad[0])
    for n in range(1, groups):
        back_sum = back_sum + mm_nt(weight[weight_rows(rep), n * wide : (n + 1) * wide], grad[n])
    back[...] = back_sum

    scaled = (node_scale * back[...]).astype(BF16)
    hss = []
    for i, d in enumerate((2, -2, -4 * toward)):
        j = REACH + d + toward
        parts[i] = mm(scaled, adj[j]).astype(BF16)
        copy = remote(parts.at[i], sibbuf.at[i], hs_s.at[i], hs_r.at[i], sibling)
        copy.start()
        hss.append(copy)

    hb_list = ((3, -4 * toward), (4, toward), (0, 2), (1, -2), (2, 4 * toward))
    for i, d in hb_list:
        mine = mm(scaled, adj[REACH + d])
        if i < 3:
            hss[i].wait_recv()
            mine = mine + sibbuf[i].astype(F32)
        outbuf[i] = mine.astype(BF16)
    own_part[...] = mm(scaled, adj[REACH]) + back[...]

    v = pre[rep]
    hidden[...] = (v * jax.nn.sigmoid(v)).astype(BF16)
    put_hidden = pltpu.make_async_copy(hidden, hidden_out, out_sem.at[0])
    put_hidden.start()

    total = core_own[y]
    for copy in ys:
        copy.wait_recv()
    for step in range(1, NY):
        total = total + y_in[(y + step) % NY].astype(F32)
    filled = piece_rows // x_rows
    x_out[0:filled] = total.astype(BF16).reshape(filled, x_rows, TILE)
    if filled < NX:
        x_out[filled:NX] = jnp.zeros((NX - filled, x_rows, TILE), BF16)
    xs = []
    for step in range(1, ZL * NX):
        to = ((xz + step) % (ZL * NX)) % NX
        copy = remote(x_out.at[to], x_in.at[xz], x_s.at[step], x_r.at[step], xz_at(step))
        copy.start()
        xs.append(copy)
    x_in[xz] = x_out[x]
    hbs = []
    for i, d in hb_list:
        copy = remote(outbuf.at[i], backbuf.at[i], hb_s.at[i], hb_r.at[i], sibling if i == 4 else blk_at(d))
        copy.start()
        hbs.append(copy)
    for copy in xs:
        copy.wait_recv()
    total = x_in[0].astype(F32)
    for g in range(1, ZL * NX):
        total = total + x_in[g].astype(F32)
    xg[x] = (total * nodes ** -0.5).astype(BF16)
    xgs = []
    for step in range(1, NX):
        copy = remote(xg.at[x], xg.at[x], xg_s.at[step], xg_r.at[step], x_at(step))
        copy.start()
        xgs.append(copy)
    for copy in xgs:
        copy.wait_recv()
    yg[y] = xg[0:filled].reshape(piece_rows, TILE)
    ygs = []
    for step in (4, 3, 5, 2, 6, 1, 7) if NY == 8 else range(1, NY):
        copy = remote(yg.at[y], yg.at[y], yg_s.at[step], yg_r.at[step], y_at(step))
        copy.start()
        ygs.append((step, copy))
    cgs = []
    puts = []

    def place(i):
        lane = core * (pieces // 2 * TILE) + (i // 2) * TILE
        at = (
            pl.ds(pl.multiple_of((i % 2) * piece_rows, piece_rows), piece_rows),
            pl.ds(pl.multiple_of(lane, TILE), TILE),
        )
        return wgrad_out.at[at]

    def pass_on(at, step):
        copy = remote(yg.at[at], place(at), cg_s.at[step], cg_r.at[step], sibling)
        copy.start()
        cgs.append(copy)
        copy = pltpu.make_async_copy(yg.at[at], place(at), out_sem.at[2 + step])
        copy.start()
        puts.append(copy)

    pass_on(y, 0)

    for step, copy in sorted(ygs, key=lambda pair: min(pair[0], NY - pair[0])):
        copy.wait_recv()
        pass_on((y + NY - step) % NY, step)

    for copy in hbs:
        copy.wait_recv()
    total = own_part[...]
    for i in range(5):
        total = total + backbuf[i].astype(F32)
    fgrad[...] = total.astype(BF16)
    put_fgrad = pltpu.make_async_copy(fgrad, fgrad_out, out_sem.at[1])
    put_fgrad.start()

    for copy in cgs + puts:
        copy.wait()
    put_hidden.wait()
    put_fgrad.wait()
    gathers = halo[0] + halo[1] + to_sibling[0] + to_sibling[1] + cots + aggs[0] + aggs[1] + relays
    for copy in gathers + core_copies + ys + hss + hbs + xs + xgs:
        copy.wait_send()
    for _, copy in ygs:
        copy.wait_send()


def finish(
    hidden_in, wgrad_in, fgrad_in, hidden_out, wgrad_out, fgrad_out, hidden, fgrad, narrow, wgrad, in_sem, out_sem
):
    cuts = 4
    depth = wgrad.shape[0] // cuts
    parts = [pl.ds(i * depth, depth) for i in range(cuts)]
    loads = [pltpu.make_async_copy(wgrad_in.at[at], narrow.at[at], in_sem.at[i]) for i, at in enumerate(parts)]
    loads.append(pltpu.make_async_copy(hidden_in, hidden, in_sem.at[cuts]))
    loads.append(pltpu.make_async_copy(fgrad_in, fgrad, in_sem.at[cuts + 1]))
    for copy in loads:
        copy.start()
    stores = [pltpu.make_async_copy(wgrad.at[at], wgrad_out.at[at], out_sem.at[i]) for i, at in enumerate(parts)]
    stores.append(pltpu.make_async_copy(hidden, hidden_out, out_sem.at[cuts]))
    stores.append(pltpu.make_async_copy(fgrad, fgrad_out, out_sem.at[cuts + 1]))
    for i in range(cuts + 2):
        loads[i].wait()
        if i < cuts:
            wgrad[parts[i], :] = narrow[parts[i], :].astype(F32)
        stores[i].start()
    for copy in stores:
        copy.wait()


def body(features, weight, cotangent, tile_val, tile_row, tile_col, tile_count):
    rows, panel = features.shape
    slots = tile_val.shape[1]
    reps = lax.axis_size("rep")
    nodes = rows * lax.axis_size("blk")
    f_in, hid = weight.shape
    wide = cotangent.shape[1]
    pieces = hid // TILE
    piece_rows = panel // 2
    x_rows = SUB * (-(-piece_rows // (SUB * NX)))
    group = ZL * NX
    vmem = pltpu.VMEM
    smem = pltpu.SMEM
    dma = pltpu.SemaphoreType.DMA
    scratch = [
        smem((1, slots), jnp.int32),
        smem((1, slots), jnp.int32),
        smem((1,), jnp.int32),
        vmem((f_in, hid), BF16),
        vmem((slots, TILE, TILE), BF16),
        vmem((WIDE, panel, rows), BF16),
        vmem((slots + 1, TILE, TILE), F32),
        vmem((WIDE, rows, rows), BF16),
        vmem((8, rows), F32),
        vmem((TILE, rows), F32),
        vmem((reps, panel, rows), BF16),
        vmem((reps, rows, wide), F32),
        vmem((reps, rows, wide), BF16),
        vmem((reps, rows, wide), BF16),
        vmem((rows, wide), BF16),
        vmem((panel, rows), F32),
        vmem((panel, rows), F32),
        vmem((3, panel, rows), BF16),
        vmem((3, panel, rows), BF16),
        vmem((5, panel, rows), BF16),
        vmem((5, panel, rows), BF16),
        vmem((panel, rows), BF16),
        vmem((pieces, piece_rows, TILE), BF16),
        vmem((pieces, piece_rows, TILE), BF16),
        vmem((pieces, piece_rows, TILE), F32),
        vmem((pieces, piece_rows, TILE), BF16),
        vmem((pieces, piece_rows, TILE), BF16),
        vmem((NX, x_rows, TILE), BF16),
        vmem((group, x_rows, TILE), BF16),
        vmem((NX, x_rows, TILE), BF16),
        vmem((pieces, piece_rows, TILE), BF16),
    ] + [
        dma((n,))
        for n in (
            7, 8, 8, 8, 8, 4, 4, 6, 6, 2, 2,
            NY, NY, group, group, NX, NX, NY, NY, NY, NY, 3, 3, 5, 5, 2 + NY,
        )
    ]
    anywhere = pl.BlockSpec(memory_space=pl.ANY)
    hbm = pl.BlockSpec(memory_space=pltpu.HBM)
    results = pl.pallas_call(
        functools.partial(kernel, nodes, slots, reps),
        out_shape=(
            jax.ShapeDtypeStruct((rows, wide), BF16),
            jax.ShapeDtypeStruct((panel, hid), BF16),
            jax.ShapeDtypeStruct((panel, rows), BF16),
        ),
        in_specs=[hbm] * 7,
        out_specs=(anywhere,) * 3,
        scratch_shapes=scratch,
        compiler_params=pltpu.CompilerParams(
            collective_id=0, has_side_effects=True, vmem_limit_bytes=VMEM_BYTES
        ),
    )(features.T, weight, cotangent, tile_val, tile_row, tile_col, tile_count)
    hidden, weight_grad, feature_grad = pl.pallas_call(
        finish,
        out_shape=(
            jax.ShapeDtypeStruct((rows, wide), BF16),
            jax.ShapeDtypeStruct((panel, hid), F32),
            jax.ShapeDtypeStruct((panel, rows), BF16),
        ),
        in_specs=[hbm] * 3,
        out_specs=(hbm,) * 3,
        scratch_shapes=[
            vmem((rows, wide), BF16),
            vmem((panel, rows), BF16),
            vmem((panel, hid), BF16),
            vmem((panel, hid), F32),
            dma((6,)),
            dma((6,)),
        ],
        compiler_params=pltpu.CompilerParams(vmem_limit_bytes=VMEM_BYTES),
    )(*results)
    return hidden, weight_grad, feature_grad.T


def solution(mesh):
    placed = (
        P("blk", "rep"),
        P(),
        P("blk", "rep"),
        P("blk", None, None, None),
        P("blk", None),
        P("blk", None),
        P("blk"),
    )
    return jax.shard_map(
        body,
        mesh=mesh,
        in_specs=placed,
        out_specs=(P("blk", "rep"), P("rep", None), P("blk", "rep")),
        check_vma=False,
    )
```

```python
import functools

import jax
import jax.numpy as jnp
from jax import lax
from jax.experimental import pallas as pl
from jax.experimental.pallas import tpu as pltpu
from jax.sharding import PartitionSpec as P

TILE = 128
ROWT = 2
REACH = 4
WIDE = 2 * REACH + 1
ZL, NY, NX, NC = 2, 8, 8, 2
SUB = 16
VMEM_BYTES = 60 * 1024 * 1024
F32 = jnp.float32
BF16 = jnp.bfloat16


def mm(a, b):
    return jnp.dot(a, b, preferred_element_type=F32)


def mm_nt(a, b):
    return lax.dot_general(a, b, (((1,), (1,)), ((), ())), preferred_element_type=F32)


def remote(src, dst, send, recv, where):
    return pltpu.make_async_remote_copy(
        src_ref=src, dst_ref=dst, send_sem=send, recv_sem=recv,
        device_id=where, device_id_type=pl.DeviceIdType.MESH,
    )


def kernel(
    nodes, slots, reps,
    feat_hbm, weight_hbm, cot_hbm, val_hbm, row_hbm, col_hbm, count_hbm,
    hidden_out, wgrad_out, fgrad_out,
    row_ref, col_ref, count_ref,
    weight, vals, win, chain, adj, scale, acc,
    aggbuf, pre, cotbuf, grad, hidden, back, own_part, parts, sibbuf, outbuf, backbuf, fgrad,
    core_out, core_in, core_own, y_out, y_in, x_out, x_in, xg, yg,
    local_sem, halo_s, halo_r, pass_s, pass_r, cot_s, cot_r, agg_s, agg_r, core_s, core_r,
    y_s, y_r, x_s, x_r, xg_s, xg_r, yg_s, yg_r, cg_s, cg_r, hs_s, hs_r, hb_s, hb_r, out_sem,
):
    blk = lax.axis_index("blk")
    rep = lax.axis_index("rep")
    blocks = ZL * NY * NX * NC
    core = blk % NC
    x = (blk // NC) % NX
    y = (blk // (NC * NX)) % NY
    zl = blk // (NC * NX * NY)
    xz = zl * NX + x
    toward = 1 - 2 * core
    panel = win.shape[1]
    pieces, piece_rows, _ = core_out.shape
    x_rows = x_out.shape[1]

    def blk_at(offset):
        return {"blk": (blk + offset + blocks) % blocks}

    def y_at(step):
        return {"blk": ((zl * NY + (y + step) % NY) * NX + x) * NC + core}

    def x_at(step):
        return {"blk": ((zl * NY + y) * NX + (x + step) % NX) * NC + core}

    def xz_at(step):
        g = (xz + step) % (ZL * NX)
        return {"blk": (((g // NX) * NY + y) * NX + g % NX) * NC + core}

    def rep_at(step):
        return {"rep": (rep + step) % reps}

    sibling = {"blk": blk + toward}
    greet_at = [blk_at(d) for d in (-4, -2, 2, 4)] + [sibling]

    get_feat = pltpu.make_async_copy(feat_hbm, win.at[REACH], local_sem.at[0])
    get_feat.start()
    get_cot = pltpu.make_async_copy(cot_hbm, cotbuf.at[rep], local_sem.at[1])
    get_cot.start()

    barrier = pltpu.get_barrier_semaphore()

    def greet(where):
        pl.semaphore_signal(barrier, inc=1, device_id=where, device_id_type=pl.DeviceIdType.MESH)

    for where in greet_at:
        greet(where)
    for step in (1, -1):
        greet(rep_at(step + reps))
    for step in range(1, NY):
        greet(y_at(step))
    for step in range(1, ZL * NX):
        greet(xz_at(step))
    greeted = len(greet_at) + 2 + NY - 1 + ZL * NX - 1

    get_rows = pltpu.make_async_copy(row_hbm, row_ref, local_sem.at[2])
    get_cols = pltpu.make_async_copy(col_hbm, col_ref, local_sem.at[3])
    get_count = pltpu.make_async_copy(count_hbm, count_ref, local_sem.at[4])
    get_vals = pltpu.make_async_copy(val_hbm.at[0], vals, local_sem.at[5])
    get_weight = pltpu.make_async_copy(weight_hbm, weight, local_sem.at[6])
    for copy in (get_rows, get_cols, get_count, get_vals, get_weight):
        copy.start()
    get_feat.wait()
    get_cot.wait()
    get_rows.wait()
    get_cols.wait()
    get_count.wait()

    count = count_ref[0]
    keys = [jnp.where(s < count, row_ref[0, s] * (WIDE * ROWT) + col_ref[0, s], -1 - s) for s in range(slots)]
    rows = [jnp.where(s < count, row_ref[0, s], -1) for s in range(slots)]
    chain[slots] = jnp.zeros((TILE, TILE), F32)

    pl.semaphore_wait(barrier, greeted)

    rows_half = panel // 2
    parts_of = [pl.ds(h * rows_half, rows_half) for h in range(2)]
    near = (-4 * toward, 2, -2, 4 * toward)
    halo = [[], []]
    to_sibling = [[], []]
    for h in range(2):
        own = win.at[REACH, parts_of[h]]
        for i, d in enumerate(near):
            copy = remote(own, win.at[REACH - d, parts_of[h]], halo_s.at[4 * h + i], halo_r.at[4 * h + i], blk_at(d))
            copy.start()
            halo[h].append(copy)
        copy = remote(own, win.at[REACH - toward, parts_of[h]], pass_s.at[4 * h + 3], pass_r.at[4 * h + 3], sibling)
        copy.start()
        to_sibling[h].append(copy)

    cots = []
    for i, step in enumerate((1, -1)):
        copy = remote(cotbuf.at[rep], cotbuf.at[rep], cot_s.at[i], cot_r.at[i], rep_at(step + reps))
        copy.start()
        cots.append(copy)

    get_vals.wait()
    chunk = 32

    def one_where(cond):
        return jnp.where(cond, 1.0, 0.0).astype(F32)

    for s in range(slots):
        before = jnp.int32(slots)
        for t in range(s):
            before = jnp.where(keys[t] == keys[s], t, before)
        v = vals[s].astype(F32)
        chain[s] = v + chain[before]

    @pl.loop(0, TILE // chunk)
    def _(c):
        at = pl.ds(pl.multiple_of(c * chunk, chunk), chunk)
        sums = [jnp.zeros((chunk, TILE), F32) for _ in range(ROWT)]
        for s in range(slots):
            v = vals[s, at, :].astype(F32)
            sq = v * v
            for r in range(ROWT):
                sums[r] = sums[r] + sq * one_where(rows[s] == r)
        for r in range(ROWT):
            acc[pl.ds(pl.multiple_of(c * chunk, chunk), chunk), r * TILE : (r + 1) * TILE] = sums[r]

    for r in range(ROWT):
        row_sq = jnp.sum(acc[0:TILE, r * TILE : (r + 1) * TILE].T, axis=0, keepdims=True)
        scale[:, r * TILE : (r + 1) * TILE] = jnp.broadcast_to(lax.rsqrt(1.0 + row_sq), (8, TILE))

    @pl.loop(0, WIDE)
    def _(j):
        for r in range(ROWT):
            for t in range(ROWT):
                last = jnp.int32(slots)
                for s in range(slots):
                    last = jnp.where(keys[s] == r * (WIDE * ROWT) + j * ROWT + t, s, last)
                adj[j, r * TILE : (r + 1) * TILE, t * TILE : (t + 1) * TILE] = chain[last].astype(BF16)

    node_scale = scale[0:1, :]
    aggs = [[], []]
    for h in range(2):
        total = mm_nt(win[REACH, parts_of[h], :], adj[REACH])
        for i in (1, 2, 0):
            d = near[i]
            halo[h][i].wait_recv()
            copy = remote(
                win.at[REACH - d, parts_of[h]], win.at[REACH - d - toward, parts_of[h]],
                pass_s.at[4 * h + i], pass_r.at[4 * h + i], sibling,
            )
            copy.start()
            to_sibling[h].append(copy)
        halo[h][3].wait_recv()
        for d in (-4, -2, 2, 4):
            total = total + mm_nt(win[REACH + d, parts_of[h], :], adj[REACH + d])
        for copy in to_sibling[h]:
            copy.wait_recv()
        for d in (-3, -1, 1, 3):
            total = total + mm_nt(win[REACH + d, parts_of[h], :], adj[REACH + d])
        aggbuf[rep, parts_of[h], :] = (win[REACH, parts_of[h], :].astype(F32) + node_scale * total).astype(BF16)
        for i, step in enumerate((1, -1)):
            at = aggbuf.at[rep, parts_of[h]]
            copy = remote(at, at, agg_s.at[2 * h + i], agg_r.at[2 * h + i], rep_at(step + reps))
            copy.start()
            aggs[h].append(copy)
        if h == 0:
            half = cotbuf.shape[1] // 2
            for i, step in enumerate((1, -1)):
                cots[i].wait_recv()
                at = cotbuf.at[(rep - step + reps) % reps, pl.ds(i * half, half)]
                copy = remote(at, at, cot_s.at[2 + i], cot_r.at[2 + i], rep_at(step + reps))
                copy.start()
                cots.append(copy)

    relays = []

    def relay(i, step):
        aggs[i][i].wait_recv()
        at = aggbuf.at[(rep - step + reps) % reps, parts_of[i]]
        copy = remote(at, at, agg_s.at[4 + i], agg_r.at[4 + i], rep_at(step + reps))
        copy.start()
        relays.append(copy)

    relay(0, 1)
    get_weight.wait()
    groups = pre.shape[0]
    wide = pre.shape[2]

    def weight_rows(q):
        return pl.ds(pl.multiple_of(q * panel, 64), panel)

    def add_pre(q, first):
        lhs = aggbuf[q].astype(F32).T.astype(BF16)
        for n in range(groups):
            part = mm(lhs, weight[weight_rows(q), n * wide : (n + 1) * wide])
            if first:
                pre[n] = part
            else:
                pre[n] += part

    add_pre(rep, True)
    relay(1, -1)
    aggs[1][0].wait_recv()
    add_pre((rep + reps - 1) % reps, False)
    aggs[0][1].wait_recv()
    add_pre((rep + 1) % reps, False)
    for copy in cots[2:] + relays:
        copy.wait_recv()
    last = (rep + 2) % reps
    last_lhs = aggbuf[last].astype(F32).T.astype(BF16)

    def grad_at(n):
        v = pre[n] + mm(last_lhs, weight[weight_rows(last), pl.ds(pl.multiple_of(n * wide, wide), wide)])
        pre[n] = v
        sig = jax.nn.sigmoid(v)
        slope = sig * (1.0 + v * (1.0 - sig))
        grad[n] = (cotbuf[n].astype(F32) * slope).astype(BF16)

    def weight_part(n, u, out):
        part = mm(aggbuf[rep], grad[n]).astype(out.dtype)
        for t in range(wide // TILE):
            for h in range(2):
                out[(u * (wide // TILE) + t) * 2 + h] = part[
                    h * piece_rows : (h + 1) * piece_rows, t * TILE : (t + 1) * TILE
                ]

    half = groups // 2
    share = pieces // half
    core_copies = []
    for u in range(half):
        n = (1 - core) * half + u
        grad_at(n)
        weight_part(n, u, core_out)
        at = pl.ds(u * share, share)
        copy = remote(core_out.at[at], core_in.at[at], core_s.at[u], core_r.at[u], sibling)
        copy.start()
        core_copies.append(copy)
    for u in range(half):
        n = core * half + u
        grad_at(n)
        weight_part(n, u, core_own)

    for u in range(half):
        core_copies[u].wait_recv()
        for i in range(u * share, (u + 1) * share):
            total = core_own[i] + core_in[i].astype(F32)
            core_own[i] = total
            y_out[i] = total.astype(BF16)
    ys = []
    for step in (4, 3, 5, 2, 6, 1, 7) if NY == 8 else range(1, NY):
        copy = remote(y_out.at[(y + step) % NY], y_in.at[y], y_s.at[step], y_r.at[step], y_at(step))
        copy.start()
        ys.append(copy)

    back_sum = mm_nt(weight[weight_rows(rep), 0:wide], grad[0])
    for n in range(1, groups):
        back_sum = back_sum + mm_nt(weight[weight_rows(rep), n * wide : (n + 1) * wide], grad[n])
    back[...] = back_sum

    scaled = (node_scale * back[...]).astype(BF16)
    hss = []
    for i, d in enumerate((2, -2, -4 * toward)):
        j = REACH + d + toward
        parts[i] = mm(scaled, adj[j]).astype(BF16)
        copy = remote(parts.at[i], sibbuf.at[i], hs_s.at[i], hs_r.at[i], sibling)
        copy.start()
        hss.append(copy)

    hb_list = ((3, -4 * toward), (4, toward), (0, 2), (1, -2), (2, 4 * toward))
    for i, d in hb_list:
        mine = mm(scaled, adj[REACH + d])
        if i < 3:
            hss[i].wait_recv()
            mine = mine + sibbuf[i].astype(F32)
        outbuf[i] = mine.astype(BF16)
    own_part[...] = mm(scaled, adj[REACH]) + back[...]

    total = core_own[y]
    for copy in ys:
        copy.wait_recv()
    for step in range(1, NY):
        total = total + y_in[(y + step) % NY].astype(F32)
    filled = piece_rows // x_rows
    x_out[0:filled] = total.astype(BF16).reshape(filled, x_rows, TILE)
    if filled < NX:
        x_out[filled:NX] = jnp.zeros((NX - filled, x_rows, TILE), BF16)
    xs = []
    for step in range(1, ZL * NX):
        to = ((xz + step) % (ZL * NX)) % NX
        copy = remote(x_out.at[to], x_in.at[xz], x_s.at[step], x_r.at[step], xz_at(step))
        copy.start()
        xs.append(copy)
    x_in[xz] = x_out[x]
    hbs = []
    for i, d in hb_list:
        copy = remote(outbuf.at[i], backbuf.at[i], hb_s.at[i], hb_r.at[i], sibling if i == 4 else blk_at(d))
        copy.start()
        hbs.append(copy)
    v = pre[rep]
    hidden[...] = (v * jax.nn.sigmoid(v)).astype(BF16)
    put_hidden = pltpu.make_async_copy(hidden, hidden_out, out_sem.at[0])
    put_hidden.start()
    for copy in xs:
        copy.wait_recv()
    total = x_in[0].astype(F32)
    for g in range(1, ZL * NX):
        total = total + x_in[g].astype(F32)
    xg[x] = (total * nodes ** -0.5).astype(BF16)
    xgs = []
    for step in range(1, NX):
        copy = remote(xg.at[x], xg.at[x], xg_s.at[step], xg_r.at[step], x_at(step))
        copy.start()
        xgs.append(copy)
    for copy in xgs:
        copy.wait_recv()
    yg[y] = xg[0:filled].reshape(piece_rows, TILE)
    ygs = []
    for step in (4, 3, 5, 2, 6, 1, 7) if NY == 8 else range(1, NY):
        copy = remote(yg.at[y], yg.at[y], yg_s.at[step], yg_r.at[step], y_at(step))
        copy.start()
        ygs.append((step, copy))
    cgs = []
    puts = []

    def place(i):
        lane = core * (pieces // 2 * TILE) + (i // 2) * TILE
        at = (
            pl.ds(pl.multiple_of((i % 2) * piece_rows, piece_rows), piece_rows),
            pl.ds(pl.multiple_of(lane, TILE), TILE),
        )
        return wgrad_out.at[at]

    def pass_on(at, step):
        copy = remote(yg.at[at], place(at), cg_s.at[step], cg_r.at[step], sibling)
        copy.start()
        cgs.append(copy)
        copy = pltpu.make_async_copy(yg.at[at], place(at), out_sem.at[2 + step])
        copy.start()
        puts.append(copy)

    pass_on(y, 0)

    for step, copy in sorted(ygs, key=lambda pair: min(pair[0], NY - pair[0])):
        copy.wait_recv()
        pass_on((y + NY - step) % NY, step)

    for copy in hbs:
        copy.wait_recv()
    total = own_part[...]
    for i in range(5):
        total = total + backbuf[i].astype(F32)
    fgrad[...] = total.astype(BF16)
    put_fgrad = pltpu.make_async_copy(fgrad, fgrad_out, out_sem.at[1])
    put_fgrad.start()

    for copy in cgs + puts:
        copy.wait()
    put_hidden.wait()
    put_fgrad.wait()
    gathers = halo[0] + halo[1] + to_sibling[0] + to_sibling[1] + cots + aggs[0] + aggs[1] + relays
    for copy in gathers + core_copies + ys + hss + hbs + xs + xgs:
        copy.wait_send()
    for _, copy in ygs:
        copy.wait_send()


def finish(
    hidden_in, wgrad_in, fgrad_in, hidden_out, wgrad_out, fgrad_out, hidden, fgrad, narrow, wgrad, in_sem, out_sem
):
    cuts = 4
    depth = wgrad.shape[0] // cuts
    parts = [pl.ds(i * depth, depth) for i in range(cuts)]
    loads = [pltpu.make_async_copy(wgrad_in.at[at], narrow.at[at], in_sem.at[i]) for i, at in enumerate(parts)]
    loads.append(pltpu.make_async_copy(hidden_in, hidden, in_sem.at[cuts]))
    loads.append(pltpu.make_async_copy(fgrad_in, fgrad, in_sem.at[cuts + 1]))
    for copy in loads:
        copy.start()
    stores = [pltpu.make_async_copy(wgrad.at[at], wgrad_out.at[at], out_sem.at[i]) for i, at in enumerate(parts)]
    stores.append(pltpu.make_async_copy(hidden, hidden_out, out_sem.at[cuts]))
    stores.append(pltpu.make_async_copy(fgrad, fgrad_out, out_sem.at[cuts + 1]))
    for i in range(cuts + 2):
        loads[i].wait()
        if i < cuts:
            wgrad[parts[i], :] = narrow[parts[i], :].astype(F32)
        stores[i].start()
    for copy in stores:
        copy.wait()


def body(features, weight, cotangent, tile_val, tile_row, tile_col, tile_count):
    rows, panel = features.shape
    slots = tile_val.shape[1]
    reps = lax.axis_size("rep")
    nodes = rows * lax.axis_size("blk")
    f_in, hid = weight.shape
    wide = cotangent.shape[1]
    pieces = hid // TILE
    piece_rows = panel // 2
    x_rows = SUB * (-(-piece_rows // (SUB * NX)))
    group = ZL * NX
    vmem = pltpu.VMEM
    smem = pltpu.SMEM
    dma = pltpu.SemaphoreType.DMA
    scratch = [
        smem((1, slots), jnp.int32),
        smem((1, slots), jnp.int32),
        smem((1,), jnp.int32),
        vmem((f_in, hid), BF16),
        vmem((slots, TILE, TILE), BF16),
        vmem((WIDE, panel, rows), BF16),
        vmem((slots + 1, TILE, TILE), F32),
        vmem((WIDE, rows, rows), BF16),
        vmem((8, rows), F32),
        vmem((TILE, rows), F32),
        vmem((reps, panel, rows), BF16),
        vmem((reps, rows, wide), F32),
        vmem((reps, rows, wide), BF16),
        vmem((reps, rows, wide), BF16),
        vmem((rows, wide), BF16),
        vmem((panel, rows), F32),
        vmem((panel, rows), F32),
        vmem((3, panel, rows), BF16),
        vmem((3, panel, rows), BF16),
        vmem((5, panel, rows), BF16),
        vmem((5, panel, rows), BF16),
        vmem((panel, rows), BF16),
        vmem((pieces, piece_rows, TILE), BF16),
        vmem((pieces, piece_rows, TILE), BF16),
        vmem((pieces, piece_rows, TILE), F32),
        vmem((pieces, piece_rows, TILE), BF16),
        vmem((pieces, piece_rows, TILE), BF16),
        vmem((NX, x_rows, TILE), BF16),
        vmem((group, x_rows, TILE), BF16),
        vmem((NX, x_rows, TILE), BF16),
        vmem((pieces, piece_rows, TILE), BF16),
    ] + [
        dma((n,))
        for n in (
            7, 8, 8, 8, 8, 4, 4, 6, 6, 2, 2,
            NY, NY, group, group, NX, NX, NY, NY, NY, NY, 3, 3, 5, 5, 2 + NY,
        )
    ]
    anywhere = pl.BlockSpec(memory_space=pl.ANY)
    hbm = pl.BlockSpec(memory_space=pltpu.HBM)
    results = pl.pallas_call(
        functools.partial(kernel, nodes, slots, reps),
        out_shape=(
            jax.ShapeDtypeStruct((rows, wide), BF16),
            jax.ShapeDtypeStruct((panel, hid), BF16),
            jax.ShapeDtypeStruct((panel, rows), BF16),
        ),
        in_specs=[hbm] * 7,
        out_specs=(anywhere,) * 3,
        scratch_shapes=scratch,
        compiler_params=pltpu.CompilerParams(
            collective_id=0, has_side_effects=True, vmem_limit_bytes=VMEM_BYTES
        ),
    )(features.T, weight, cotangent, tile_val, tile_row, tile_col, tile_count)
    hidden, weight_grad, feature_grad = pl.pallas_call(
        finish,
        out_shape=(
            jax.ShapeDtypeStruct((rows, wide), BF16),
            jax.ShapeDtypeStruct((panel, hid), F32),
            jax.ShapeDtypeStruct((panel, rows), BF16),
        ),
        in_specs=[hbm] * 3,
        out_specs=(hbm,) * 3,
        scratch_shapes=[
            vmem((rows, wide), BF16),
            vmem((panel, rows), BF16),
            vmem((panel, hid), BF16),
            vmem((panel, hid), F32),
            dma((6,)),
            dma((6,)),
        ],
        compiler_params=pltpu.CompilerParams(vmem_limit_bytes=VMEM_BYTES),
    )(*results)
    return hidden, weight_grad, feature_grad.T


def solution(mesh):
    placed = (
        P("blk", "rep"),
        P(),
        P("blk", "rep"),
        P("blk", None, None, None),
        P("blk", None),
        P("blk", None),
        P("blk"),
    )
    return jax.shard_map(
        body,
        mesh=mesh,
        in_specs=placed,
        out_specs=(P("blk", "rep"), P("rep", None), P("blk", "rep")),
        check_vma=False,
    )
```
